128 devices in a mesh: island: 8 (over z_lo, y), fsdp: 16 (over z_hi, x, core).
Axes of the slice: x: 4, y: 4, z: 4 (z_hi: 2, z_lo: 2; z = z_hi * 2 + z_lo), core: 2. Of those that a mesh axis runs over, the one named last changes fastest.
Arguments:
- weights: bfloat16 [4096, 14336], P(None, 'fsdp'), may hold values from -3 to 3
- momentum: bfloat16 [4096, 14336], P(None, 'fsdp'), may hold values from -0.59765625 to 0.59765625
- table: bfloat16 [2048, 4096], P(None, 'fsdp'), may hold values from -6 to 6
- token_ids: int32 [8, 2, 896], P('island'), may hold values from 0 to 2047
- cotangent: bfloat16 [8, 2, 896, 14336], P('island', None, None, 'fsdp'), may hold values from -6 to 6
Outputs:
- new_weights: bfloat16 [4096, 14336], P(None, 'fsdp')
The draws below stay inside these ranges and needn't reach their ends.
All inputs are finite; a program needn't handle non-finite values.
Results may differ from the reference program's by a relative error of at most 0.005.
Values may be sent and summed in bfloat16 or wider, within the bound.
No kernel may reach another device: no remote copies, remote signals or barrier semaphores. Data moves between devices by JAX's collectives and lax.ppermute only.
A program may use at most 128 MiB of HBM per device.

```python
import math
import jax
import jax.numpy as jnp
from jax import lax

D = 4096
FF = 14336
TOK = 896
ROWS = 2048
STEPS = 2
ISLANDS = 8
N_ISLAND = 8


def touch_ends(values, own_key, low, largest):
    place = [jax.random.randint(jax.random.fold_in(own_key, axis), (), 0, length) for axis, length in enumerate(values.shape)]
    longest = values.shape.index(max(values.shape))
    next_to = place[:longest] + [(place[longest] + 1) % values.shape[longest]] + place[longest + 1:]
    return values.at[tuple(place)].set(low).at[tuple(next_to)].set(largest)


def block_scale(stream_key, extent, split, smallest, high):
    loudness = 1.0
    for position, parts in split:
        heights = jax.random.uniform(jax.random.fold_in(jax.random.fold_in(stream_key, 6), position), (parts,), jnp.float32, smallest / len(split), high / len(split))
        loudness = loudness * jnp.repeat(jnp.exp(heights), extent[position] // parts).reshape((-1,) + (1,) * (len(extent) - 1 - position))
    return loudness


def gaussian(key, shape, deviation, reach, shards=(), kind=jnp.bfloat16):
    loudness = block_scale(key, shape, shards, -0.22, 0.18) if shards else 1.0
    array = jax.random.normal(key, shape, jnp.float32) * deviation * loudness
    return jnp.minimum(jnp.maximum(array, -reach), reach).astype(kind)


def setup_inputs(seed: int = 0) -> dict:
    streams_of = jax.random.split(jax.random.key(seed), 6)
    weights = gaussian(streams_of[0], (D, FF), 0.5, 3.0, ((1, 16),))
    momentum = gaussian(streams_of[1], (D, FF), 0.1, 0.59765625, ((1, 16),))
    table = gaussian(streams_of[2], (ROWS, D), 1.0, 6.0, ((1, 16),))
    token_ids = touch_ends(jax.random.randint(streams_of[3], (ISLANDS, STEPS, TOK), 0, ROWS), jax.random.fold_in(streams_of[3], 1), 0, ROWS - 1).astype(jnp.int32)
    cotangent = gaussian(streams_of[4], (ISLANDS, STEPS, TOK, FF), 1.0, 6.0, ((0, 8), (3, 16)))
    return dict(weights=weights, momentum=momentum, table=table, token_ids=token_ids, cotangent=cotangent)


beta_one = 0.9
beta_two = 0.95
adam_eps = 0.0001
inner_rate = 0.1
decay_rate = 0.1
outer_rate = 0.7
outer_moment = 0.9

def silu_slope(hidden):
    sigma = jax.nn.sigmoid(hidden)
    return sigma * (1.0 + hidden * (1.0 - sigma))

def island_delta(weights, table, island_ids, island_cot):
    scale = 1.0 / math.sqrt(D)
    start = weights.astype(jnp.float32)
    local = start
    first = jnp.zeros((D, FF), jnp.float32)
    second = jnp.zeros((D, FF), jnp.float32)
    for step in range(STEPS):
        work = weights if step == 0 else local.astype(jnp.bfloat16)
        inputs = jnp.take(table, island_ids[step], axis=0)
        hidden = jnp.dot(inputs, work, preferred_element_type=jnp.float32) * scale
        upstream = (island_cot[step].astype(jnp.float32) * silu_slope(hidden) / TOK).astype(jnp.bfloat16)
        grad = jnp.dot(inputs.T, upstream, preferred_element_type=jnp.float32) * scale
        first = beta_one * first + (1.0 - beta_one) * grad
        second = beta_two * second + (1.0 - beta_two) * grad * grad
        m_hat = first / (1.0 - beta_one ** (step + 1))
        v_hat = second / (1.0 - beta_two ** (step + 1))
        local = local - inner_rate * (m_hat / (jnp.sqrt(v_hat) + adam_eps) + decay_rate * local)
    return (start - local).astype(jnp.bfloat16).astype(jnp.float32)

def reference(weights, momentum, table, token_ids, cotangent):

    def add_island(index, total):
        return total + island_delta(weights, table, token_ids[index], cotangent[index])
    total = lax.fori_loop(0, N_ISLAND, add_island, jnp.zeros((D, FF), jnp.float32))
    mean = total / N_ISLAND
    moment = outer_moment * momentum.astype(jnp.float32) + mean
    fresh = weights.astype(jnp.float32) - outer_rate * (mean + outer_moment * moment)
    return fresh.astype(jnp.bfloat16)
```

```python
import math

import jax
import jax.numpy as jnp
from jax import lax
from jax.experimental import pallas as pl
from jax.experimental.pallas import tpu as pltpu
from jax.sharding import PartitionSpec as P

beta_one = 0.9
beta_two = 0.95
adam_eps = 0.0001
inner_rate = 0.1
decay_rate = 0.1
outer_rate = 0.7
outer_moment = 0.9

MB = 1 << 20
AXES = ("island", "fsdp")
XA, XB = 1, 3
SPLIT = (64, 48)
ROWS_Y = 768
PARTS = ((0, 1408), (1408, 1408), (2816, 1280))
ORDERS = ((1, 3, 4), (3, 4, 1), (4, 1, 3))


def swap(a, partner):
    pairs = []
    for zlo in range(2):
        for y in range(4):
            for zhi in range(2):
                for x in range(4):
                    for c in range(2):
                        px, py, pz, pc = partner(x, y, zhi * 2 + zlo, c)
                        me = (zlo * 4 + y) * 16 + zhi * 8 + x * 2 + c
                        to = ((pz % 2) * 4 + py) * 16 + (pz // 2) * 8 + px * 2 + pc
                        pairs.append((me, to))
    return lax.ppermute(a, AXES, pairs)


def over_x(a, first):
    return swap(a, lambda x, y, z, c: (x ^ (XA if (c == 0) == first else XB), y, z, c))


def over_y(a, first):
    return swap(a, lambda x, y, z, c: (x, y ^ (XA if (c == 0) == first else XB), z, c))


def over_z(a):
    return swap(a, lambda x, y, z, c: (x, y, z ^ 3, c))


def over_core(a):
    return swap(a, lambda x, y, z, c: (x, y, z, c ^ 1))


def over_island(a, mask):
    return swap(a, lambda x, y, z, c: (x, y ^ (mask & 3), z ^ (mask >> 2), c))


def slope(hidden):
    sigma = 0.5 * (1.0 + jnp.tanh(0.5 * hidden))
    return sigma * (1.0 + hidden * (1.0 - sigma))


def gather_table(table, island, fsdp):
    rows, width = table.shape
    x, core, zhi, y = (fsdp // 2) % 4, fsdp % 2, fsdp // 8, island % 4
    span = ROWS_Y // 4
    part_y = lax.dynamic_slice(table, (y * span, 0), (span, width))
    part_x = table[ROWS_Y:]
    y0 = jnp.concatenate([part_y, over_z(part_y)])
    x_z = over_z(part_x)
    y1 = over_x(y0, True)
    y2 = over_x(jnp.concatenate([y0, y1]), False)
    x1 = over_x(part_x, True)
    x1z = over_x(x_z, True)
    x2 = over_x(jnp.concatenate([part_x, x1]), False)
    x2z = over_x(jnp.concatenate([x_z, x1z]), False)
    all8 = jnp.concatenate([y0, y1, y2])
    w1 = over_y(all8, True)
    w2 = over_y(jnp.concatenate([all8, w1]), False)
    own = [table, x_z, x1, x1z, x2, x2z, all8, w1, w2]
    other = [over_core(a) for a in own]

    copies, offsets = [], []

    def place(piece, source, count, row, xx, zz, cc):
        copies.append((piece, source, count))
        offsets.append((row, 256 * (zz * 8 + xx * 2 + cc)))

    for q in range(2):
        cc = core ^ q
        d1 = jnp.where(cc == 0, XA, XB)
        d2 = XA + XB - d1
        base = 9 * q
        n = rows - ROWS_Y
        place(base, 0, rows, 0, x, zhi, cc)
        place(base + 1, 0, n, ROWS_Y, x, zhi ^ 1, cc)
        place(base + 2, 0, n, ROWS_Y, x ^ d1, zhi, cc)
        place(base + 3, 0, n, ROWS_Y, x ^ d1, zhi ^ 1, cc)
        place(base + 4, 0, n, ROWS_Y, x ^ d2, zhi, cc)
        place(base + 4, n, n, ROWS_Y, x ^ 2, zhi, cc)
        place(base + 5, 0, n, ROWS_Y, x ^ d2, zhi ^ 1, cc)
        place(base + 5, n, n, ROWS_Y, x ^ 2, zhi ^ 1, cc)
        xs = [x, x ^ d1, x ^ d2, x ^ 2]
        for piece, start, yy in (
            (base + 6, 0, y),
            (base + 7, 0, y ^ d1),
            (base + 8, 0, y ^ d2),
            (base + 8, 8 * span, y ^ 2),
        ):
            for block in range(1, 8):
                place(piece, start + block * span, span, yy * span, xs[block // 2], zhi ^ (block % 2), cc)
    where = jnp.stack([jnp.stack([jnp.asarray(v, jnp.int32) for v in pair]) for pair in offsets])

    def kernel(where_ref, *refs):
        pieces, whole, sems = refs[:18], refs[18], refs[19]
        started = []
        for i, (piece, source, count) in enumerate(copies):
            row = pl.multiple_of(where_ref[i, 0], 16)
            col = pl.multiple_of(where_ref[i, 1], 256)
            copy = pltpu.make_async_copy(
                pieces[piece].at[pl.ds(source, count), :],
                whole.at[pl.ds(row, count), pl.ds(col, 256)],
                sems.at[i],
            )
            copy.start()
            started.append(copy)
        for copy in started:
            copy.wait()

    full = width * 16
    return pl.pallas_call(
        kernel,
        in_specs=[pl.BlockSpec(memory_space=pltpu.SMEM)] + [pl.BlockSpec(memory_space=pl.ANY)] * 18,
        out_specs=pl.BlockSpec(memory_space=pltpu.VMEM),
        out_shape=pltpu.VMEM((rows, full), table.dtype),
        scratch_shapes=[pltpu.SemaphoreType.DMA((len(copies),))],
        compiler_params=pltpu.CompilerParams(vmem_limit_bytes=20 * MB),
        cost_estimate=pl.CostEstimate(flops=0, bytes_accessed=2 * rows * full * 2, transcendentals=0),
        name="gather_table",
    )(where, *own, *other)


def add_by_row(cot, ids, rows):
    count, units, tokens = cot.shape

    def kernel(cot_ref, ids_ref, *outs):
        tile = 512
        for t in range(rows // tile):
            row = lax.broadcasted_iota(jnp.int32, (tile, tokens), 0) + t * tile
            hot = jnp.where(row == ids_ref[0], 1.0, 0.0).astype(jnp.bfloat16)
            total = lax.dot_general(
                cot_ref[0], hot, (((1,), (1,)), ((), ())), preferred_element_type=jnp.float32
            ).astype(jnp.bfloat16)
            at = 0
            for out, size in zip(outs, SPLIT):
                out[0, :, t * tile : (t + 1) * tile] = total[at : at + size]
                at += size

    return pl.pallas_call(
        kernel,
        grid=(count,),
        in_specs=[
            pl.BlockSpec((1, units, tokens), lambda i: (i, 0, 0)),
            pl.BlockSpec((1, 1, tokens), lambda i: (i, 0, 0)),
        ],
        out_specs=[pl.BlockSpec((1, size, rows), lambda i: (i, 0, 0)) for size in SPLIT],
        out_shape=[jax.ShapeDtypeStruct((count, size, rows), jnp.bfloat16) for size in SPLIT],
        compiler_params=pltpu.CompilerParams(vmem_limit_bytes=24 * MB),
        cost_estimate=pl.CostEstimate(
            flops=2 * count * units * tokens * rows, bytes_accessed=count * units * (tokens + rows) * 2, transcendentals=0
        ),
        name="add_by_row",
    )(cot, ids)


def first_step(table, w, cots, tokens):
    rows, width = table.shape
    units = w.shape[0]
    scale = 1.0 / math.sqrt(width)
    block = 512

    def kernel(table_ref, w_ref, cot_ref, wb_ref, work_ref, grad_ref, up_ref):
        i = pl.program_id(0)

        @pl.when(i == 0)
        def _():
            for t in range(rows // block):
                at = slice(t * block, (t + 1) * block)
                hidden = lax.dot_general(
                    w_ref[...], table_ref[at, :], (((1,), (1,)), ((), ())), preferred_element_type=jnp.float32
                )
                factor = slope(hidden * scale) * (1.0 / tokens)
                for m in range(8):
                    up_ref[m * units : (m + 1) * units, at] = (cot_ref[m, :, at].astype(jnp.float32) * factor).astype(
                        jnp.bfloat16
                    )

        cols = pl.ds(pl.multiple_of(i * block, block), block)
        grad = jnp.dot(up_ref[...], table_ref[:, cols], preferred_element_type=jnp.float32) * scale
        grad_ref[...] = grad.astype(jnp.bfloat16)
        base = wb_ref[...].astype(jnp.float32)
        for m in range(8):
            g = grad[m * units : (m + 1) * units]
            local = base - inner_rate * (g / (jnp.abs(g) + adam_eps) + decay_rate * base)
            work_ref[m * units : (m + 1) * units, :] = local.astype(jnp.bfloat16)

    return pl.pallas_call(
        kernel,
        grid=(width // block,),
        in_specs=[
            pl.BlockSpec(memory_space=pltpu.VMEM),
            pl.BlockSpec((units, width), lambda i: (0, 0)),
            pl.BlockSpec((8, units, rows), lambda i: (0, 0, 0)),
            pl.BlockSpec((units, block), lambda i: (0, i)),
        ],
        out_specs=[pl.BlockSpec((8 * units, block), lambda i: (0, i))] * 2,
        out_shape=[jax.ShapeDtypeStruct((8 * units, width), jnp.bfloat16)] * 2,
        scratch_shapes=[pltpu.VMEM((8 * units, rows), jnp.bfloat16)],
        compiler_params=pltpu.CompilerParams(vmem_limit_bytes=36 * MB),
        cost_estimate=pl.CostEstimate(
            flops=18 * units * rows * width, bytes_accessed=rows * width * 2 + 36 * units * width, transcendentals=0
        ),
        name="first_step",
    )(table, w, cots, w)


def second_upstream(table, work, cots, tokens):
    rows, width = table.shape
    many = work.shape[0]
    scale = 1.0 / math.sqrt(width)
    block = 512

    def kernel(table_ref, work_ref, cot_ref, up_ref):
        at = pl.ds(pl.multiple_of(pl.program_id(0) * block, block), block)
        hidden = lax.dot_general(
            work_ref[...], table_ref[at, :], (((1,), (1,)), ((), ())), preferred_element_type=jnp.float32
        )
        up_ref[...] = (cot_ref[...].astype(jnp.float32) * (slope(hidden * scale) * (1.0 / tokens))).astype(jnp.bfloat16)

    return pl.pallas_call(
        kernel,
        grid=(rows // block,),
        in_specs=[
            pl.BlockSpec(memory_space=pltpu.VMEM),
            pl.BlockSpec((many, width), lambda i: (0, 0)),
            pl.BlockSpec((many, block), lambda i: (0, i)),
        ],
        out_specs=pl.BlockSpec((many, block), lambda i: (0, i)),
        out_shape=jax.ShapeDtypeStruct((many, rows), jnp.bfloat16),
        compiler_params=pltpu.CompilerParams(vmem_limit_bytes=36 * MB),
        cost_estimate=pl.CostEstimate(
            flops=2 * many * rows * width, bytes_accessed=rows * width * 2 + 2 * many * width, transcendentals=0
        ),
        name="second_upstream",
    )(table, work, cots.reshape(many, rows))


def outer_step(table, up, grads, w, momentum):
    rows, width = table.shape
    units = w.shape[0]
    scale = 1.0 / math.sqrt(width)
    block = 512

    def kernel(table_ref, up_ref, grad_ref, w_ref, mom_ref, out_ref):
        cols = pl.ds(pl.multiple_of(pl.program_id(0) * block, block), block)
        second_grad = jnp.dot(up_ref[...], table_ref[:, cols], preferred_element_type=jnp.float32) * scale
        start = w_ref[...].astype(jnp.float32)
        total = jnp.zeros(start.shape, jnp.float32)
        for m in range(8):
            span = slice(m * units, (m + 1) * units)
            g0 = grad_ref[span, :].astype(jnp.float32)
            g1 = second_grad[span]
            local = start - inner_rate * (g0 / (jnp.abs(g0) + adam_eps) + decay_rate * start)
            first = beta_one * (1.0 - beta_one) * g0 + (1.0 - beta_one) * g1
            second = beta_two * (1.0 - beta_two) * g0 * g0 + (1.0 - beta_two) * g1 * g1
            m_hat = first * (1.0 / (1.0 - beta_one**2))
            v_hat = second * (1.0 / (1.0 - beta_two**2))
            local = local - inner_rate * (m_hat / (jnp.sqrt(v_hat) + adam_eps) + decay_rate * local)
            total = total + (start - local).astype(jnp.bfloat16).astype(jnp.float32)
        mean = total * (1.0 / 8.0)
        moment = outer_moment * mom_ref[...].astype(jnp.float32) + mean
        out_ref[...] = (start - outer_rate * (mean + outer_moment * moment)).astype(jnp.bfloat16)

    return pl.pallas_call(
        kernel,
        grid=(width // block,),
        in_specs=[
            pl.BlockSpec(memory_space=pltpu.VMEM),
            pl.BlockSpec((8 * units, rows), lambda i: (0, 0)),
            pl.BlockSpec((8 * units, block), lambda i: (0, i)),
            pl.BlockSpec((units, block), lambda i: (0, i)),
            pl.BlockSpec((units, block), lambda i: (0, i)),
        ],
        out_specs=pl.BlockSpec((units, block), lambda i: (0, i)),
        out_shape=jax.ShapeDtypeStruct((units, width), jnp.bfloat16),
        compiler_params=pltpu.CompilerParams(vmem_limit_bytes=36 * MB),
        cost_estimate=pl.CostEstimate(
            flops=16 * units * rows * width, bytes_accessed=rows * width * 2 + 36 * units * width, transcendentals=0
        ),
        name="outer_step",
    )(table, up, grads, w, momentum)


def spread(new):
    found = []
    for (low, size), (e1, e2, e3) in zip(PARTS, ORDERS):
        own = new[:, low : low + size]
        r1 = over_island(own, e1)
        two = jnp.concatenate([own, r1])
        r2 = over_island(two, e2)
        r3 = over_island(jnp.concatenate([two, r2]), e3)
        found.append([(own, (0,)), (r1, (e1,)), (r2, (e2, e2 ^ e1)), (r3, (e3, e3 ^ e1, e3 ^ e2, e3 ^ e2 ^ e1))])
    return found


def assemble(chunks, island, units, width):
    operands, copies, masks = [], [[] for _ in PARTS], []
    at = 0
    for size, found in zip(SPLIT, chunks):
        for p, pieces in enumerate(found):
            for array, froms in pieces:
                for j, mask in enumerate(froms):
                    copies[p].append((len(operands), j * size, size, at, mask))
                operands.append(array)
        at += size
    total = sum(len(c) for c in copies)
    n = len(operands)
    where = jnp.stack([(island ^ m) * units for m in range(8)]).astype(jnp.int32)

    def kernel(where_ref, *refs):
        arrays, out, held, turned, sems, out_sems = refs[:n], refs[n], refs[n + 1], refs[n + 2], refs[n + 3], refs[n + 4]
        k, waits = 0, []
        for (low, length), group in zip(PARTS, copies):
            mine = []
            for piece, source, size, place, mask in group:
                row = pl.multiple_of(where_ref[mask] + place, 16)
                copy = pltpu.make_async_copy(
                    arrays[piece].at[pl.ds(source, size), :],
                    held.at[pl.ds(row, size), pl.ds(low, length)],
                    sems.at[k],
                )
                copy.start()
                mine.append(copy)
                k += 1
            waits.append(mine)
        outs = []
        for p, ((low, length), mine) in enumerate(zip(PARTS, waits)):
            for copy in mine:
                copy.wait()
            for col in range(low, low + length, 128):
                turned[col : col + 128, :] = held[:, col : col + 128].T
            copy = pltpu.make_async_copy(
                turned.at[pl.ds(low, length), :], out.at[pl.ds(low, length), :], out_sems.at[p]
            )
            copy.start()
            outs.append(copy)
        for copy in outs:
            copy.wait()

    return pl.pallas_call(
        kernel,
        in_specs=[pl.BlockSpec(memory_space=pltpu.SMEM)] + [pl.BlockSpec(memory_space=pl.ANY)] * n,
        out_specs=pl.BlockSpec(memory_space=pl.ANY),
        out_shape=jax.ShapeDtypeStruct((width, 8 * units), jnp.bfloat16),
        scratch_shapes=[
            pltpu.VMEM((8 * units, width), jnp.bfloat16),
            pltpu.VMEM((width, 8 * units), jnp.bfloat16),
            pltpu.SemaphoreType.DMA((total,)),
            pltpu.SemaphoreType.DMA((len(PARTS),)),
        ],
        compiler_params=pltpu.CompilerParams(vmem_limit_bytes=24 * MB),
        cost_estimate=pl.CostEstimate(flops=0, bytes_accessed=32 * units * width, transcendentals=0),
        name="assemble",
    )(where, *operands)


def body(weights, momentum, table, token_ids, cotangent):
    island, fsdp = lax.axis_index("island"), lax.axis_index("fsdp")
    width, hidden_units = weights.shape
    steps, tokens = token_ids.shape[1:]
    rows = table.shape[0]
    units = hidden_units // 8

    turned = jnp.swapaxes(cotangent[0], 1, 2)
    every_id = lax.all_gather(token_ids[0], "island", axis=0)
    sums = []
    for step in range(steps):
        blocks = [
            lax.dynamic_slice(turned[step], ((island ^ m) * units, 0), (units, tokens)) for m in range(8)
        ]
        arrived = jnp.stack([blocks[0]] + [over_island(blocks[m], m) for m in range(1, 8)])
        ids = jnp.stack([lax.dynamic_index_in_dim(every_id[:, step], island ^ m, 0) for m in range(8)])
        sums.append(add_by_row(arrived, ids, rows))

    def mine(a):
        return lax.dynamic_slice(a.T, (island * units, 0), (units, width))

    w, mom = mine(weights), mine(momentum)
    whole = gather_table(table, island, fsdp)
    chunks, at = [], 0
    for c, size in enumerate(SPLIT):
        w_c, mom_c = w[at : at + size], mom[at : at + size]
        work, grads = first_step(whole, w_c, sums[0][c], tokens)
        up = second_upstream(whole, work, sums[1][c], tokens)
        chunks.append(spread(outer_step(whole, up, grads, w_c, mom_c)))
        at += size
    return assemble(chunks, island, units, width)


def solution(mesh):
    placed = (
        P(None, "fsdp"),
        P(None, "fsdp"),
        P(None, "fsdp"),
        P("island", None, None),
        P("island", None, None, "fsdp"),
    )
    return jax.shard_map(body, mesh=mesh, in_specs=placed, out_specs=P(None, "fsdp"), check_vma=False)
```

```python
import math

import jax
import jax.numpy as jnp
from jax import lax
from jax.experimental import pallas as pl
from jax.experimental.pallas import tpu as pltpu
from jax.sharding import PartitionSpec as P

beta_one = 0.9
beta_two = 0.95
adam_eps = 0.0001
inner_rate = 0.1
decay_rate = 0.1
outer_rate = 0.7
outer_moment = 0.9

MB = 1 << 20
AXES = ("island", "fsdp")
XA, XB = 1, 3
DIRECT = 768
PARTS = ((0, 1408), (1408, 1408), (2816, 1280))
ORDERS = ((1, 3, 4), (3, 4, 1), (4, 1, 3))
IDS = 16


def small(**kw):
    return pl.CostEstimate(flops=0, bytes_accessed=1024, transcendentals=0)


def swap(a, partner):
    pairs = []
    for zlo in range(2):
        for y in range(4):
            for zhi in range(2):
                for x in range(4):
                    for c in range(2):
                        px, py, pz, pc = partner(x, y, zhi * 2 + zlo, c)
                        me = (zlo * 4 + y) * 16 + zhi * 8 + x * 2 + c
                        to = ((pz % 2) * 4 + py) * 16 + (pz // 2) * 8 + px * 2 + pc
                        pairs.append((me, to))
    return lax.ppermute(a, AXES, pairs)


def over_x(a, first):
    return swap(a, lambda x, y, z, c: (x ^ (XA if (c == 0) == first else XB), y, z, c))


def over_y(a, first):
    return swap(a, lambda x, y, z, c: (x, y ^ (XA if (c == 0) == first else XB), z, c))


def over_z(a):
    return swap(a, lambda x, y, z, c: (x, y, z ^ 3, c))


def over_core(a):
    return swap(a, lambda x, y, z, c: (x, y, z, c ^ 1))


def over_island(a, mask):
    return swap(a, lambda x, y, z, c: (x, y ^ (mask & 3), z ^ (mask >> 2), c))


def slope(hidden):
    sigma = 0.5 * (1.0 + jnp.tanh(0.5 * hidden))
    return sigma * (1.0 + hidden * (1.0 - sigma))


def turn_cotangent(cot, ids, island):
    steps, tokens, hidden_units = cot.shape
    units = hidden_units // 8
    where = ((island ^ jnp.arange(8)) * units).astype(jnp.int32)

    def kernel(where_ref, cot_ref, ids_ref, *refs):
        outs, held, turned, digits, in_sems, out_sems = refs[:8], refs[8], refs[9], refs[10], refs[11], refs[12]
        loads = []
        for s in range(steps):
            load = pltpu.make_async_copy(cot_ref.at[s], held.at[s], in_sems.at[s])
            load.start()
            loads.append(load)
        row = lax.broadcasted_iota(jnp.int32, (IDS, tokens), 0)
        rows = jnp.zeros((IDS, tokens), jnp.int32)
        for s in range(steps):
            one = ids_ref[s : s + 1, :]
            rows = jnp.where(row == 2 * s, one >> 8, jnp.where(row == 2 * s + 1, one & 255, rows))
        digits[...] = rows.astype(jnp.float32).astype(jnp.bfloat16)
        stores = []

        def store(source, target, k):
            copy = pltpu.make_async_copy(source, target, out_sems.at[k])
            copy.start()
            stores.append(copy)

        for m in range(8):
            store(digits, outs[m].at[pl.ds(steps * units, IDS), :], 16 + m)
        for s in range(steps):
            loads[s].wait()
            for col in range(0, hidden_units, 128):
                turned[s, col : col + 128, :] = held[s, :, col : col + 128].T
            for m in range(8):
                at = pl.multiple_of(where_ref[m], 16)
                store(turned.at[s, pl.ds(at, units), :], outs[m].at[pl.ds(s * units, units), :], 8 * s + m)
        for copy in stores:
            copy.wait()

    return pl.pallas_call(
        kernel,
        in_specs=[
            pl.BlockSpec(memory_space=pltpu.SMEM),
            pl.BlockSpec(memory_space=pltpu.HBM),
            pl.BlockSpec(memory_space=pltpu.VMEM),
        ],
        out_specs=[pl.BlockSpec(memory_space=pltpu.HBM)] * 8,
        out_shape=[jax.ShapeDtypeStruct((steps * units + IDS, tokens), cot.dtype)] * 8,
        scratch_shapes=[
            pltpu.VMEM((steps, tokens, hidden_units), cot.dtype),
            pltpu.VMEM((steps, hidden_units, tokens), cot.dtype),
            pltpu.VMEM((IDS, tokens), cot.dtype),
            pltpu.SemaphoreType.DMA((steps,)),
            pltpu.SemaphoreType.DMA((24,)),
        ],
        compiler_params=pltpu.CompilerParams(vmem_limit_bytes=60 * MB),
        cost_estimate=small(),
        name="turn_cotangent",
    )(where, cot, ids)


def own_rows(weights, momentum, island, after):
    width, hidden_units = weights.shape
    units = hidden_units // 8
    first = island * units
    low = jnp.minimum(first // 128, hidden_units // 128 - 2) * 128
    where = jnp.stack([low, first - low]).astype(jnp.int32)

    def kernel(where_ref, w_ref, m_ref, _, w_out, m_out, held, turned, sems):
        cols = pl.ds(pl.multiple_of(where_ref[0], 128), 256)
        rows = pl.ds(pl.multiple_of(where_ref[1], 16), units)
        loads = []
        for k, ref in enumerate((w_ref, m_ref)):
            load = pltpu.make_async_copy(ref.at[:, cols], held.at[k], sems.at[k])
            load.start()
            loads.append(load)
        for k, out in enumerate((w_out, m_out)):
            loads[k].wait()
            for at in range(0, width, 512):
                turned[:, at : at + 512] = held[k, at : at + 512, :].T
            out[...] = turned[rows, :]

    return pl.pallas_call(
        kernel,
        in_specs=[pl.BlockSpec(memory_space=pltpu.SMEM)] + [pl.BlockSpec(memory_space=pltpu.HBM)] * 3,
        out_specs=[pl.BlockSpec(memory_space=pltpu.VMEM)] * 2,
        out_shape=[jax.ShapeDtypeStruct((units, width), weights.dtype)] * 2,
        scratch_shapes=[
            pltpu.VMEM((2, width, 256), weights.dtype),
            pltpu.VMEM((256, width), weights.dtype),
            pltpu.SemaphoreType.DMA((2,)),
        ],
        compiler_params=pltpu.CompilerParams(vmem_limit_bytes=60 * MB),
        cost_estimate=small(),
        name="own_rows",
    )(where, weights, momentum, after)


def add_by_row(arrived, rows, step, steps, after):
    tokens = arrived[0].shape[1]
    units = (arrived[0].shape[0] - IDS) // steps
    highs = rows // 256

    def kernel(*refs):
        messages, out = refs[:8], refs[9]
        row = lax.broadcasted_iota(jnp.int32, (256, tokens), 0).astype(jnp.float32)
        for m in range(8):
            digits = messages[m][steps * units : steps * units + IDS, :].astype(jnp.float32)
            high, low = digits[2 * step : 2 * step + 1], digits[2 * step + 1 : 2 * step + 2]
            hot = jnp.where(low == row, 1.0, 0.0).astype(jnp.bfloat16)
            cot = messages[m][step * units : (step + 1) * units, :]
            parted = [cot * jnp.where(high == float(k), 1.0, 0.0).astype(jnp.bfloat16) for k in range(highs)]
            total = lax.dot_general(
                jnp.concatenate(parted), hot, (((1,), (1,)), ((), ())), preferred_element_type=jnp.float32
            ).astype(jnp.bfloat16)
            for k in range(highs):
                out[m * units : (m + 1) * units, k * 256 : (k + 1) * 256] = total[k * units : (k + 1) * units]

    return pl.pallas_call(
        kernel,
        in_specs=[pl.BlockSpec(memory_space=pltpu.VMEM)] * 8 + [pl.BlockSpec(memory_space=pltpu.HBM)],
        out_specs=pl.BlockSpec(memory_space=pltpu.VMEM),
        out_shape=jax.ShapeDtypeStruct((8 * units, rows), jnp.bfloat16),
        compiler_params=pltpu.CompilerParams(vmem_limit_bytes=24 * MB),
        cost_estimate=pl.CostEstimate(flops=4 * 10**9, bytes_accessed=7 * MB, transcendentals=0),
        name="add_by_row",
    )(*arrived, after)


def pack(pieces, after=()):
    total = sum(count for _, _, count in pieces)
    width = pieces[0][0].shape[1]
    firsts = jnp.stack([jnp.asarray(low, jnp.int32) for _, low, _ in pieces])
    n = len(pieces)

    def kernel(firsts_ref, *refs):
        out, sems = refs[n + len(after)], refs[n + len(after) + 1]
        copies, at = [], 0
        for k, (_, _, count) in enumerate(pieces):
            low = pl.multiple_of(firsts_ref[k], 16)
            copy = pltpu.make_async_copy(refs[k].at[pl.ds(low, count), :], out.at[pl.ds(at, count), :], sems.at[k])
            copy.start()
            copies.append(copy)
            at += count
        for copy in copies:
            copy.wait()

    return pl.pallas_call(
        kernel,
        in_specs=[pl.BlockSpec(memory_space=pltpu.SMEM)] + [pl.BlockSpec(memory_space=pltpu.HBM)] * (n + len(after)),
        out_specs=pl.BlockSpec(memory_space=pltpu.VMEM),
        out_shape=jax.ShapeDtypeStruct((total, width), pieces[0][0].dtype),
        scratch_shapes=[pltpu.SemaphoreType.DMA((n,))],
        compiler_params=pltpu.CompilerParams(vmem_limit_bytes=8 * MB),
        cost_estimate=small(),
        name="pack",
    )(firsts, *(array for array, _, _ in pieces), *after)


def gather_pieces(table, messages, island, beside):
    rows = table.shape[0]
    odd = island % 2
    half, left = rows // 2, (rows - DIRECT) // 2
    z = over_z(table)
    x1 = over_x(table, True)
    table_o = over_core(table)
    send = pack([(table, odd * half, half), (x1, odd * half, half)], messages[1:2])
    x2 = over_x(send, False)
    x1_o = over_core(x1)
    early = beside(0, send)
    z_kept = pack([(z, 0, rows)], [early[0]])
    x1z = over_x(z_kept, True)
    z_o = over_core(z_kept)
    y2 = over_y(x2, True)
    x2_o = over_core(x2)
    low = DIRECT + odd * left
    x2zp = over_x(pack([(z_kept, low, left), (x1z, low, left)], [x2]), False)
    send = pack([(z_kept, 0, DIRECT), (x1z, 0, DIRECT)])
    x2zd = over_x(send, False)
    x1z_o = over_core(x1z)
    y2_o = over_core(y2)
    y2z = over_y(x2zp, True)
    x2zp_o = over_core(x2zp)
    late = beside(1, x2zp)
    x2zd_o = over_core(x2zd)
    y2z_o = over_core(y2z)
    own = [table, x1, x2, y2, z_kept, x1z, x2zp, x2zd, y2z]
    other = [table_o, x1_o, x2_o, y2_o, z_o, x1z_o, x2zp_o, x2zd_o, y2z_o]
    return own + other, early, late


def places(rows, x, core, zhi, odd):
    half, left = rows // 2, (rows - DIRECT) // 2
    found = []
    for q in range(2):
        cc = core ^ q
        d1 = XA + (XB - XA) * cc
        cols = [[256 * ((zhi ^ zz) * 8 + xx * 2 + cc) for xx in (x, x ^ d1, x ^ d1 ^ 2, x ^ 2)] for zz in range(2)]
        for zz, k, piece, source, count, row in (
            (0, 0, 0, 0, rows, 0),
            (0, 1, 1, 0, rows, 0),
            (1, 0, 4, 0, rows, 0),
            (1, 1, 5, 0, rows, 0),
            (0, 2, 2, 0, half, odd * half),
            (0, 3, 2, half, half, odd * half),
            (0, 2, 3, 0, half, (1 - odd) * half),
            (0, 3, 3, half, half, (1 - odd) * half),
            (1, 2, 6, 0, left, DIRECT + odd * left),
            (1, 3, 6, left, left, DIRECT + odd * left),
            (1, 2, 7, 0, DIRECT, 0),
            (1, 3, 7, DIRECT, DIRECT, 0),
            (1, 2, 8, 0, left, DIRECT + (1 - odd) * left),
            (1, 3, 8, left, left, DIRECT + (1 - odd) * left),
        ):
            found.append((zz * 2 + k if k < 2 else 2 + zz * 2 + k, q, 9 * q + piece, source, count, row, cols[zz][k]))
    return sorted(found, key=lambda entry: entry[0])


def main_steps(pieces, position, w, momentum, cots, tokens):
    rows = cots[0].shape[1]
    units, width = w.shape
    many = 8 * units
    scale = 1.0 / math.sqrt(width)
    eps = adam_eps / scale
    first_0 = beta_one * (1.0 - beta_one) / (1.0 - beta_one**2)
    first_1 = (1.0 - beta_one) / (1.0 - beta_one**2)
    second_0 = beta_two * (1.0 - beta_two) / (1.0 - beta_two**2)
    second_1 = (1.0 - beta_two) / (1.0 - beta_two**2)
    keep = 1.0 - inner_rate * decay_rate
    block = 512
    n = len(pieces)
    n_copies = 28

    def kernel(where_ref, *refs):
        piece_refs, (w_hbm, mom_hbm, c0_hbm, c1_hbm), outs = refs[:n], refs[n : n + 4], refs[n + 4 : n + 7]
        table, work, grads, up, cot, ratio, hidden, w_ref, mom_ref, out_ref, sems, more = refs[n + 7 :]
        flat = places(rows, *(where_ref[k] for k in range(4)))

        def start(source, target, sem):
            copy = pltpu.make_async_copy(source, target, sem)
            copy.start()
            return copy

        load_w = start(w_hbm, w_ref, more.at[0])
        copies = []
        for k, (_, _, piece, source, count, row, col) in enumerate(flat):
            row, col = pl.multiple_of(row, 16), pl.multiple_of(col, 256)
            copies.append(
                start(
                    piece_refs[piece].at[pl.ds(source, count), :],
                    table.at[pl.ds(row, count), pl.ds(col, 256)],
                    sems.at[k],
                )
            )
            if k == n_copies // 2:
                load_c = start(c0_hbm, cot, more.at[1])
                load_m = start(mom_hbm, mom_ref, more.at[2])
        load_w.wait()
        for g in range(8):
            for k in range(n_copies):
                if flat[k][0] == g:
                    copies[k].wait()
            for q in range(2):
                col = next(entry[6] for entry in flat if entry[:2] == (g, q))
                cols = pl.ds(pl.multiple_of(col, 256), 256)
                part = lax.dot_general(
                    w_ref[:, cols], table[:, cols], (((1,), (1,)), ((), ())), preferred_element_type=jnp.float32
                )
                if g == 0 and q == 0:
                    hidden[...] = part
                else:
                    hidden[...] += part
        load_c.wait()
        for at in range(0, rows, block):
            cols = slice(at, at + block)
            factor = slope(hidden[:, cols] * scale) * (1.0 / tokens)
            for m in range(8):
                span = slice(m * units, (m + 1) * units)
                up[span, cols] = (cot[span, cols].astype(jnp.float32) * factor).astype(jnp.bfloat16)
        load_c = start(c1_hbm, cot, more.at[1])

        @pl.loop(0, width // block)
        def _(i):
            cols = pl.ds(pl.multiple_of(i * block, block), block)
            grad = jnp.dot(up[...], table[:, cols], preferred_element_type=jnp.float32)
            kept = w_ref[:, cols].astype(jnp.float32) * keep
            total = jnp.zeros(kept.shape, jnp.float32)
            for m in range(8):
                span = slice(m * units, (m + 1) * units)
                g = grad[span]
                r = g * pl.reciprocal(jnp.abs(g) + eps, approx=True)
                total = total + r
                work[span, cols] = (kept - inner_rate * r).astype(jnp.bfloat16)
                grads[span, cols] = g.astype(jnp.bfloat16)
            ratio[:, cols] = total

        load_c.wait()

        @pl.loop(0, rows // block)
        def _(t):
            at = pl.ds(pl.multiple_of(t * block, block), block)
            h = lax.dot_general(
                work[...], table[at, :], (((1,), (1,)), ((), ())), preferred_element_type=jnp.float32
            )
            up[:, at] = (cot[:, at].astype(jnp.float32) * (slope(h * scale) * (1.0 / tokens))).astype(jnp.bfloat16)

        load_m.wait()

        @pl.loop(0, width // block)
        def _(i):
            cols = pl.ds(pl.multiple_of(i * block, block), block)
            grad = jnp.dot(up[...], table[:, cols], preferred_element_type=jnp.float32)
            start_w = w_ref[:, cols].astype(jnp.float32)
            total = jnp.zeros(start_w.shape, jnp.float32)
            for m in range(8):
                span = slice(m * units, (m + 1) * units)
                g1 = grad[span]
                g0 = grads[span, cols].astype(jnp.float32)
                v = (second_0 * g0) * g0 + (second_1 * g1) * g1 + 1e-30
                total = total + (first_0 * g0 + first_1 * g1) * pl.reciprocal(v * lax.rsqrt(v) + eps, approx=True)
            mean = (1.0 - keep * keep) * start_w + (inner_rate / 8.0) * (keep * ratio[:, cols] + total)
            moment = outer_moment * mom_ref[:, cols].astype(jnp.float32) + mean
            out_ref[:, cols] = (start_w - outer_rate * (mean + outer_moment * moment)).astype(jnp.bfloat16)

        for out, (low, size) in zip(outs, PARTS):
            out[...] = out_ref[:, low : low + size]

    return pl.pallas_call(
        kernel,
        in_specs=[pl.BlockSpec(memory_space=pltpu.SMEM)] + [pl.BlockSpec(memory_space=pltpu.HBM)] * (n + 4),
        out_specs=[pl.BlockSpec(memory_space=pltpu.VMEM)] * 3,
        out_shape=[jax.ShapeDtypeStruct((units, size), jnp.bfloat16) for _, size in PARTS],
        scratch_shapes=[
            pltpu.VMEM((rows, width), jnp.bfloat16),
            pltpu.VMEM((many, width), jnp.bfloat16),
            pltpu.VMEM((many, width), jnp.bfloat16),
            pltpu.VMEM((many, rows), jnp.bfloat16),
            pltpu.VMEM((many, rows), jnp.bfloat16),
            pltpu.VMEM((units, width), jnp.float32),
            pltpu.VMEM((units, rows), jnp.float32),
            pltpu.VMEM((units, width), jnp.bfloat16),
            pltpu.VMEM((units, width), jnp.bfloat16),
            pltpu.VMEM((units, width), jnp.bfloat16),
            pltpu.SemaphoreType.DMA((n_copies,)),
            pltpu.SemaphoreType.DMA((3,)),
        ],
        compiler_params=pltpu.CompilerParams(vmem_limit_bytes=60 * MB),
        cost_estimate=pl.CostEstimate(flops=52 * units * rows * width, bytes_accessed=rows * width * 2, transcendentals=0),
        name="main_steps",
    )(position, *pieces, w, momentum, *cots)


def spread(new):
    held = [[(part, 0)] for part in new]
    for step in range(3):
        sends = [part[0][0] if step == 0 else jnp.concatenate([block for block, _ in part]) for part in held]
        sends = lax.optimization_barrier(tuple(sends))
        for part, order, send in zip(held, ORDERS, sends):
            part.append((over_island(send, order[step]), step))
    found = []
    for part, (e1, e2, e3) in zip(held, ORDERS):
        own, r1, r2, r3 = (block for block, _ in part)
        found.append([(own, (0,)), (r1, (e1,)), (r2, (e2, e2 ^ e1)), (r3, (e3, e3 ^ e1, e3 ^ e2, e3 ^ e2 ^ e1))])
    return found


def assemble(found, island, units, width):
    operands, copies = [], [[] for _ in PARTS]
    for p, pieces in enumerate(found):
        for array, froms in pieces:
            for j, mask in enumerate(froms):
                copies[p].append((len(operands), j * units, units, 0, mask))
            operands.append(array)
    total = sum(len(c) for c in copies)
    n = len(operands)
    where = jnp.stack([(island ^ m) * units for m in range(8)]).astype(jnp.int32)

    def kernel(where_ref, *refs):
        arrays, out, held, turned, sems, out_sems = refs[:n], refs[n], refs[n + 1], refs[n + 2], refs[n + 3], refs[n + 4]
        k, waits = 0, []
        for (low, length), group in zip(PARTS, copies):
            mine = []
            for piece, source, size, place, mask in group:
                row = pl.multiple_of(where_ref[mask] + place, 16)
                copy = pltpu.make_async_copy(
                    arrays[piece].at[pl.ds(source, size), :],
                    held.at[pl.ds(row, size), pl.ds(low, length)],
                    sems.at[k],
                )
                copy.start()
                mine.append(copy)
                k += 1
            waits.append(mine)
        outs = []
        for p, ((low, length), mine) in enumerate(zip(PARTS, waits)):
            for copy in mine:
                copy.wait()
            for col in range(low, low + length, 128):
                turned[col : col + 128, :] = held[:, col : col + 128].T
            copy = pltpu.make_async_copy(
                turned.at[pl.ds(low, length), :], out.at[pl.ds(low, length), :], out_sems.at[p]
            )
            copy.start()
            outs.append(copy)
        for copy in outs:
            copy.wait()

    return pl.pallas_call(
        kernel,
        in_specs=[pl.BlockSpec(memory_space=pltpu.SMEM)] + [pl.BlockSpec(memory_space=pltpu.HBM)] * n,
        out_specs=pl.BlockSpec(memory_space=pltpu.HBM),
        out_shape=jax.ShapeDtypeStruct((width, 8 * units), jnp.bfloat16),
        scratch_shapes=[
            pltpu.VMEM((8 * units, width), jnp.bfloat16),
            pltpu.VMEM((width, 8 * units), jnp.bfloat16),
            pltpu.SemaphoreType.DMA((total,)),
            pltpu.SemaphoreType.DMA((len(PARTS),)),
        ],
        compiler_params=pltpu.CompilerParams(vmem_limit_bytes=24 * MB),
        cost_estimate=pl.CostEstimate(flops=0, bytes_accessed=32 * units * width, transcendentals=0),
        name="assemble",
    )(where, *operands)


def body(weights, momentum, table, token_ids, cotangent):
    island, fsdp = lax.axis_index("island"), lax.axis_index("fsdp")
    width, hidden_units = weights.shape
    steps, tokens = token_ids.shape[1:]
    rows = table.shape[0]
    units = hidden_units // 8
    messages = turn_cotangent(cotangent[0], token_ids[0], island)
    arrived = [messages[0]] + [over_island(messages[m], m) for m in range(1, 8)]
    def beside(part, after):
        if part == 0:
            return own_rows(weights, momentum, island, after)
        return [add_by_row(arrived, rows, step, steps, after) for step in range(steps)]

    pieces, (w, mom), cots = gather_pieces(table, messages, island, beside)
    position = jnp.stack([(fsdp // 2) % 4, fsdp % 2, fsdp // 8, island % 2]).astype(jnp.int32)
    new = main_steps(pieces, position, w, mom, cots, tokens)
    return assemble(spread(new), island, units, width)


def solution(mesh):
    placed = (
        P(None, "fsdp"),
        P(None, "fsdp"),
        P(None, "fsdp"),
        P("island", None, None),
        P("island", None, None, "fsdp"),
    )
    return jax.shard_map(body, mesh=mesh, in_specs=placed, out_specs=P(None, "fsdp"), check_vma=False)
```

```python
import math

import jax
import jax.numpy as jnp
from jax import lax
from jax.experimental import pallas as pl
from jax.experimental.pallas import tpu as pltpu
from jax.sharding import PartitionSpec as P

beta_one = 0.9
beta_two = 0.95
adam_eps = 0.0001
inner_rate = 0.1
decay_rate = 0.1
outer_rate = 0.7
outer_moment = 0.9

MB = 1 << 20
AXES = ("island", "fsdp")
XA, XB = 1, 3
MASKS = ((0, 2, 1, 4, 6, 3, 5, 7), (0, 2, 3, 4, 6, 1, 7, 5))
PARTS = ((0, 1408), (1408, 1408), (2816, 1280))
LINKS = (1, 3, 4)
VMEM_ALL = 64 * MB - 256 * 1024
IDS = 16


X, CORE, ZHI, ODD, LOW, SHIFT, ODD_ROWS, PARTNERS, ISLANDS = 0, 1, 2, 3, 4, 5, 6, 8, 16


def scalars(island, fsdp, units, rows):
    masks = jnp.where(fsdp % 2 == 0, jnp.asarray(MASKS[0]), jnp.asarray(MASKS[1]))
    low = jnp.minimum(island * units // 128, 8 * units // 128 - 2) * 128
    single = [(fsdp // 2) % 4, fsdp % 2, fsdp // 8, island % 2, low, island * units - low, (island % 2) * (rows // 2), 0]
    return jnp.concatenate(
        [jnp.stack([jnp.asarray(v, jnp.int32) for v in single]), (island ^ masks) * units, (island ^ jnp.arange(8)) * units]
    ).astype(jnp.int32)


def small():
    return pl.CostEstimate(flops=0, bytes_accessed=1024, transcendentals=0)


def swap(a, partner):
    pairs = []
    for zlo in range(2):
        for y in range(4):
            for zhi in range(2):
                for x in range(4):
                    for c in range(2):
                        px, py, pz, pc = partner(x, y, zhi * 2 + zlo, c)
                        me = (zlo * 4 + y) * 16 + zhi * 8 + x * 2 + c
                        to = ((pz % 2) * 4 + py) * 16 + (pz // 2) * 8 + px * 2 + pc
                        pairs.append((me, to))
    return lax.ppermute(a, AXES, pairs)


def over_x(a, first):
    return swap(a, lambda x, y, z, c: (x ^ (XA if (c == 0) == first else XB), y, z, c))


def over_y(a, first):
    return swap(a, lambda x, y, z, c: (x, y ^ (XA if (c == 0) == first else XB), z, c))


def over_z(a):
    return swap(a, lambda x, y, z, c: (x, y, z ^ 3, c))


def over_core(a):
    return swap(a, lambda x, y, z, c: (x, y, z, c ^ 1))


def over_island(a, mask, other=None):
    masks = (mask, mask if other is None else other)
    return swap(a, lambda x, y, z, c: (x, y ^ (masks[c] & 3), z ^ (masks[c] >> 2), c))


def slope(product, scale, factor):
    half = product * (0.5 * scale)
    bent = jnp.tanh(half)
    return (bent * (0.5 * factor) + 0.5 * factor) * (1.0 + half * (1.0 - bent))


def turn_cotangent(where, cot, ids):
    steps, tokens, hidden_units = cot.shape
    units = hidden_units // 8
    n = 8

    def kernel(where_ref, cot_ref, ids_ref, *refs):
        outs, held, turned, digits, in_sems, out_sems = refs[:n], *refs[n:]
        loads = []
        for s in range(steps):
            load = pltpu.make_async_copy(cot_ref.at[s], held.at[s], in_sems.at[s])
            load.start()
            loads.append(load)
        row = lax.broadcasted_iota(jnp.int32, (IDS, tokens), 0)
        rows = jnp.zeros((IDS, tokens), jnp.int32)
        for s in range(steps):
            one = ids_ref[s : s + 1, :]
            rows = jnp.where(row == 2 * s, one >> 8, jnp.where(row == 2 * s + 1, one & 255, rows))
        digits[...] = rows.astype(jnp.float32).astype(jnp.bfloat16)
        stores = []

        def store(source, target):
            copy = pltpu.make_async_copy(source, target, out_sems.at[len(stores)])
            copy.start()
            stores.append(copy)

        for m in range(n):
            store(digits, outs[m].at[pl.ds(steps * units, IDS), :])
        for s in range(steps):
            loads[s].wait()
            for col in range(0, hidden_units, 128):
                turned[s, col : col + 128, :] = held[s, :, col : col + 128].T
            for m in range(n):
                at = pl.multiple_of(where_ref[PARTNERS + m], 16)
                store(turned.at[s, pl.ds(at, units), :], outs[m].at[pl.ds(s * units, units), :])
        for copy in stores:
            copy.wait()

    return pl.pallas_call(
        kernel,
        in_specs=[
            pl.BlockSpec(memory_space=pltpu.SMEM),
            pl.BlockSpec(memory_space=pltpu.HBM),
            pl.BlockSpec(memory_space=pltpu.VMEM),
        ],
        out_specs=[pl.BlockSpec(memory_space=pltpu.HBM)] * n,
        out_shape=[jax.ShapeDtypeStruct((steps * units + IDS, tokens), cot.dtype)] * n,
        scratch_shapes=[
            pltpu.VMEM((steps, tokens, hidden_units), cot.dtype),
            pltpu.VMEM((steps, hidden_units, tokens), cot.dtype),
            pltpu.VMEM((IDS, tokens), cot.dtype),
            pltpu.SemaphoreType.DMA((steps,)),
            pltpu.SemaphoreType.DMA((n * (steps + 1),)),
        ],
        compiler_params=pltpu.CompilerParams(vmem_limit_bytes=VMEM_ALL),
        cost_estimate=small(),
        name="turn_cotangent",
    )(where, cot, ids)


def own_rows(where, weights, momentum, after):
    width, hidden_units = weights.shape
    units = hidden_units // 8

    def kernel(where_ref, w_ref, m_ref, _, w_out, m_out, held, turned, sems):
        stores = []
        cols = pl.ds(pl.multiple_of(where_ref[LOW], 128), 256)
        rows = pl.ds(pl.multiple_of(where_ref[SHIFT], 16), units)
        loads = []
        for k, ref in enumerate((w_ref, m_ref)):
            load = pltpu.make_async_copy(ref.at[:, cols], held.at[k], sems.at[k])
            load.start()
            loads.append(load)
        for k, out in enumerate((w_out, m_out)):
            loads[k].wait()
            for at in range(0, width, 512):
                turned[k, :, at : at + 512] = held[k, at : at + 512, :].T
            store = pltpu.make_async_copy(turned.at[k, rows, :], out, sems.at[2 + k])
            store.start()
            stores.append(store)
        for store in stores:
            store.wait()

    return pl.pallas_call(
        kernel,
        in_specs=[pl.BlockSpec(memory_space=pltpu.SMEM)] + [pl.BlockSpec(memory_space=pltpu.HBM)] * 3,
        out_specs=[pl.BlockSpec(memory_space=pltpu.HBM)] * 2,
        out_shape=[jax.ShapeDtypeStruct((units, width), weights.dtype)] * 2,
        scratch_shapes=[
            pltpu.VMEM((2, width, 256), weights.dtype),
            pltpu.VMEM((2, 256, width), weights.dtype),
            pltpu.SemaphoreType.DMA((4,)),
        ],
        compiler_params=pltpu.CompilerParams(vmem_limit_bytes=VMEM_ALL),
        cost_estimate=small(),
        name="own_rows",
    )(where, weights, momentum, *after)


def add_by_row(arrived, rows, steps):
    n = len(arrived)
    tokens = arrived[0].shape[1]
    units = (arrived[0].shape[0] - IDS) // steps
    highs = rows // 256

    def kernel(*refs):
        sources, targets, messages, sums, in_sems, out_sems = refs[:n], refs[n : n + steps], *refs[n + steps :]
        loads = [pltpu.make_async_copy(sources[m], messages.at[m], in_sems.at[m]) for m in range(n)]
        for load in loads:
            load.start()
        stores = []
        row = lax.broadcasted_iota(jnp.int32, (256, tokens), 0).astype(jnp.float32)
        for m in range(n):
            loads[m].wait()
            digits = messages[m, steps * units : steps * units + IDS, :].astype(jnp.float32)
            for step in range(steps):
                high, low = digits[2 * step : 2 * step + 1], digits[2 * step + 1 : 2 * step + 2]
                hot = jnp.where(low == row, 1.0, 0.0).astype(jnp.bfloat16)
                cot = messages[m, step * units : (step + 1) * units, :]
                parted = [cot * jnp.where(high == float(k), 1.0, 0.0).astype(jnp.bfloat16) for k in range(highs)]
                total = lax.dot_general(
                    jnp.concatenate(parted), hot, (((1,), (1,)), ((), ())), preferred_element_type=jnp.float32
                ).astype(jnp.bfloat16)
                for k in range(highs):
                    sums[m, step, :, k * 256 : (k + 1) * 256] = total[k * units : (k + 1) * units]
                store = pltpu.make_async_copy(
                    sums.at[m, step], targets[step].at[pl.ds(m * units, units), :], out_sems.at[m * steps + step]
                )
                store.start()
                stores.append(store)
        for store in stores:
            store.wait()

    return pl.pallas_call(
        kernel,
        in_specs=[pl.BlockSpec(memory_space=pltpu.HBM)] * n,
        out_specs=[pl.BlockSpec(memory_space=pltpu.HBM)] * steps,
        out_shape=[jax.ShapeDtypeStruct((n * units, rows), jnp.bfloat16)] * steps,
        scratch_shapes=[
            pltpu.VMEM((n, *arrived[0].shape), jnp.bfloat16),
            pltpu.VMEM((n, steps, units, rows), jnp.bfloat16),
            pltpu.SemaphoreType.DMA((n,)),
            pltpu.SemaphoreType.DMA((n * steps,)),
        ],
        compiler_params=pltpu.CompilerParams(vmem_limit_bytes=VMEM_ALL),
        cost_estimate=pl.CostEstimate(flops=n * 10**9, bytes_accessed=n * MB, transcendentals=0),
        name="add_by_row",
    )(*arrived)


def together(*arrays):
    n = len(arrays)
    return pl.pallas_call(
        lambda *refs: None,
        in_specs=[pl.BlockSpec(memory_space=pltpu.HBM)] * n,
        out_specs=[pl.BlockSpec(memory_space=pltpu.HBM)] * n,
        out_shape=[jax.ShapeDtypeStruct(a.shape, a.dtype) for a in arrays],
        input_output_aliases={k: k for k in range(n)},
        compiler_params=pltpu.CompilerParams(vmem_limit_bytes=VMEM_ALL),
        cost_estimate=small(),
        name="together",
    )(*arrays)


def pack(where, pieces):
    total = sum(count for _, _, count in pieces)
    width = pieces[0][0].shape[1]
    n = len(pieces)

    def kernel(where_ref, *refs):
        out, held, in_sems, out_sems = refs[n:]
        loads, stores, at = [], [], 0
        for k, (_, scalar, count) in enumerate(pieces):
            low = 0 if scalar is None else pl.multiple_of(where_ref[scalar], 16)
            here = pl.ds(at, count)
            loads.append(pltpu.make_async_copy(refs[k].at[pl.ds(low, count), :], held.at[here, :], in_sems.at[k]))
            stores.append(pltpu.make_async_copy(held.at[here, :], out.at[here, :], out_sems.at[k]))
            loads[k].start()
            at += count
        for load, store in zip(loads, stores):
            load.wait()
            store.start()
        for store in stores:
            store.wait()

    return pl.pallas_call(
        kernel,
        in_specs=[pl.BlockSpec(memory_space=pltpu.SMEM)] + [pl.BlockSpec(memory_space=pltpu.HBM)] * n,
        out_specs=pl.BlockSpec(memory_space=pltpu.HBM),
        out_shape=jax.ShapeDtypeStruct((total, width), pieces[0][0].dtype),
        scratch_shapes=[
            pltpu.VMEM((total, width), pieces[0][0].dtype),
            pltpu.SemaphoreType.DMA((n,)),
            pltpu.SemaphoreType.DMA((n,)),
        ],
        compiler_params=pltpu.CompilerParams(vmem_limit_bytes=VMEM_ALL),
        cost_estimate=small(),
        name="pack",
    )(where, *(array for array, _, _ in pieces))


def places(rows, x, core, zhi, odd):
    half = rows // 2
    found = []
    for q in range(2):
        cc = core ^ q
        d1 = XA + (XB - XA) * cc
        cols = [[256 * ((zhi ^ zz) * 8 + xx * 2 + cc) for xx in (x, x ^ d1, x ^ d1 ^ 2, x ^ 2)] for zz in range(2)]
        for zz, k, piece, source, count, row in (
            (0, 0, 0, 0, rows, 0),
            (0, 1, 1, 0, rows, 0),
            (1, 0, 4, 0, rows, 0),
            (1, 1, 5, 0, rows, 0),
            (0, 2, 2, 0, half, odd * half),
            (0, 3, 2, half, half, odd * half),
            (0, 2, 3, 0, half, (1 - odd) * half),
            (0, 3, 3, half, half, (1 - odd) * half),
            (1, 2, 6, 0, rows, 0),
            (1, 3, 6, rows, rows, 0),
        ):
            found.append((zz * 2 + k if k < 2 else 2 + zz * 2 + k, q, 7 * q + piece, source, count, row, cols[zz][k]))
    return sorted(found, key=lambda entry: entry[0])


def main_steps(pieces, position, w, momentum, cots, tokens):
    rows = cots[0][0].shape[1]
    units, width = w.shape
    many = 8 * units
    scale = 1.0 / math.sqrt(width)
    first_0 = beta_one * (1.0 - beta_one) / (1.0 - beta_one**2)
    first_1 = (1.0 - beta_one) / (1.0 - beta_one**2)
    root_0 = math.sqrt(beta_two * (1.0 - beta_two) / (1.0 - beta_two**2))
    root_1 = math.sqrt((1.0 - beta_two) / (1.0 - beta_two**2))
    weight_0, weight_1 = first_0 / root_0, first_1 / root_1
    eps = adam_eps / scale
    narrow = jnp.bfloat16
    keep = 1.0 - inner_rate * decay_rate
    block = 1024
    n, sets = len(pieces), len(cots)
    n_copies = 20

    def kernel(where_ref, *refs):
        piece_refs, (w_hbm, mom_hbm), refs = refs[:n], refs[n : n + 2], refs[n + 2 :]
        cot_hbm, out_ref, refs = refs[: 2 * sets], refs[2 * sets], refs[2 * sets + 1 :]
        table, work, grads, up, cot, ratio, hidden, w_ref, mom_ref, sems, more = refs
        flat = places(rows, *(where_ref[k] for k in (X, CORE, ZHI, ODD)))

        def start(source, target, sem):
            copy = pltpu.make_async_copy(source, target, sem)
            copy.start()
            return copy

        def load_cots(step):
            loads, at = [], 0
            for k in range(sets):
                size = cots[k][step].shape[0]
                loads.append(start(cot_hbm[2 * k + step], cot.at[pl.ds(at, size), :], more.at[2 + k]))
                at += size
            return loads

        load_w = start(w_hbm, w_ref, more.at[0])
        copies = []
        for k, (_, _, piece, source, count, row, col) in enumerate(flat):
            row, col = pl.multiple_of(row, 16), pl.multiple_of(col, 256)
            copies.append(
                start(
                    piece_refs[piece].at[pl.ds(source, count), :],
                    table.at[pl.ds(row, count), pl.ds(col, 256)],
                    sems.at[k],
                )
            )
            if k == n_copies // 2:
                load_c = load_cots(0)
                load_m = start(mom_hbm, mom_ref, more.at[1])
        load_w.wait()
        for g in range(8):
            for k in range(n_copies):
                if flat[k][0] == g:
                    copies[k].wait()
            for q in range(2):
                col = next(entry[6] for entry in flat if entry[:2] == (g, q))
                cols = pl.ds(pl.multiple_of(col, 256), 256)
                part = lax.dot_general(
                    w_ref[:, cols], table[:, cols], (((1,), (1,)), ((), ())), preferred_element_type=jnp.float32
                )
                if g == 0 and q == 0:
                    hidden[...] = part
                else:
                    hidden[...] += part
        for load in load_c:
            load.wait()
        for at in range(0, rows, block):
            cols = slice(at, at + block)
            factor = slope(hidden[:, cols], scale, root_0 / tokens)
            for m in range(8):
                span = slice(m * units, (m + 1) * units)
                up[span, cols] = (cot[span, cols].astype(jnp.float32) * factor).astype(jnp.bfloat16)
        load_c = load_cots(1)

        @pl.loop(0, width // block)
        def _(i):
            cols = pl.ds(pl.multiple_of(i * block, block), block)
            grad = jnp.dot(up[...], table[:, cols], preferred_element_type=jnp.float32)
            kept = w_ref[:, cols].astype(jnp.float32) * keep
            total = jnp.zeros(kept.shape, jnp.float32)
            for m in range(8):
                span = slice(m * units, (m + 1) * units)
                g = grad[span]
                r = g * pl.reciprocal(jnp.abs(g) + eps * root_0, approx=True)
                total = total + r
                work[span, cols] = (kept - inner_rate * r).astype(jnp.bfloat16)
                grads[span, cols] = g.astype(jnp.bfloat16)
            ratio[:, cols] = total

        for load in load_c:
            load.wait()

        @pl.loop(0, rows // block)
        def _(t):
            at = pl.ds(pl.multiple_of(t * block, block), block)
            h = lax.dot_general(
                work[...], table[at, :], (((1,), (1,)), ((), ())), preferred_element_type=jnp.float32
            )
            up[:, at] = (cot[:, at].astype(jnp.float32) * slope(h, scale, root_1 / tokens)).astype(jnp.bfloat16)

        load_m.wait()

        @pl.loop(0, width // block)
        def _(i):
            cols = pl.ds(pl.multiple_of(i * block, block), block)
            grad = jnp.dot(up[...], table[:, cols], preferred_element_type=jnp.float32)
            start_w = w_ref[:, cols].astype(jnp.float32)
            total = jnp.zeros(start_w.shape, jnp.float32)
            for m in range(8):
                span = slice(m * units, (m + 1) * units)
                b = grad[span].astype(narrow)
                a = grads[span, cols]
                v = a * a + b * b + narrow(1e-30)
                r = (a + narrow(weight_1 / weight_0) * b) * pl.reciprocal(
                    v * lax.rsqrt(v) + narrow(eps), approx=True
                )
                total = total + r.astype(jnp.float32)
            mean = (1.0 - keep * keep) * start_w + (inner_rate / 8.0) * (keep * ratio[:, cols] + weight_0 * total)
            moment = outer_moment * mom_ref[:, cols].astype(jnp.float32) + mean
            out_ref[:, cols] = (start_w - outer_rate * (mean + outer_moment * moment)).astype(jnp.bfloat16)

    return pl.pallas_call(
        kernel,
        in_specs=[pl.BlockSpec(memory_space=pltpu.SMEM)] + [pl.BlockSpec(memory_space=pltpu.HBM)] * (n + 2 + 2 * sets),
        out_specs=pl.BlockSpec(memory_space=pltpu.VMEM),
        out_shape=jax.ShapeDtypeStruct((units, width), jnp.bfloat16),
        scratch_shapes=[
            pltpu.VMEM((rows, width), jnp.bfloat16),
            pltpu.VMEM((many, width), jnp.bfloat16),
            pltpu.VMEM((many, width), jnp.bfloat16),
            pltpu.VMEM((many, rows), jnp.bfloat16),
            pltpu.VMEM((many, rows), jnp.bfloat16),
            pltpu.VMEM((units, width), jnp.float32),
            pltpu.VMEM((units, rows), jnp.float32),
            pltpu.VMEM((units, width), jnp.bfloat16),
            pltpu.VMEM((units, width), jnp.bfloat16),
            pltpu.SemaphoreType.DMA((n_copies,)),
            pltpu.SemaphoreType.DMA((2 + sets,)),
        ],
        compiler_params=pltpu.CompilerParams(vmem_limit_bytes=VMEM_ALL),
        cost_estimate=pl.CostEstimate(flops=52 * units * rows * width, bytes_accessed=rows * width * 2, transcendentals=0),
        name="main_steps",
    )(position, *pieces, w, momentum, *(c for pair in cots for c in pair))


def spread(new):
    e1, e2, e3 = LINKS
    near = [over_island(new, e) for e in LINKS]
    far = [over_island(near[1], e1), over_island(near[2], e2), over_island(near[0], e3)]
    found = [(new, 0, 0), (near[0], 0, e1), (near[1], 0, e2), (near[2], 0, e3)]
    found += [(far[0], 0, e1 ^ e2), (far[1], 0, e2 ^ e3), (far[2], 0, e1 ^ e3)]
    for (low, size), source, e in zip(PARTS, (far[1], far[2], far[0]), LINKS):
        found.append((over_island(source[:, low : low + size], e), low, e1 ^ e2 ^ e3))
    return found


def assemble(found, where, units, width):
    n = len(found)

    def kernel(where_ref, *refs):
        arrays, out, held, turned, sems, out_sems = refs[:n], refs[n], refs[n + 1], refs[n + 2], refs[n + 3], refs[n + 4]
        copies = []
        for k, (array, low, mask) in enumerate(found):
            row = pl.multiple_of(where_ref[ISLANDS + mask], 16)
            copy = pltpu.make_async_copy(
                arrays[k], held.at[pl.ds(row, units), pl.ds(low, array.shape[1])], sems.at[k]
            )
            copy.start()
            copies.append(copy)
        for copy in copies:
            copy.wait()
        outs = []
        for p, (low, length) in enumerate(PARTS):
            for col in range(low, low + length, 128):
                turned[col : col + 128, :] = held[:, col : col + 128].T
            copy = pltpu.make_async_copy(
                turned.at[pl.ds(low, length), :], out.at[pl.ds(low, length), :], out_sems.at[p]
            )
            copy.start()
            outs.append(copy)
        for copy in outs:
            copy.wait()

    return pl.pallas_call(
        kernel,
        in_specs=[pl.BlockSpec(memory_space=pltpu.SMEM)] + [pl.BlockSpec(memory_space=pltpu.HBM)] * n,
        out_specs=pl.BlockSpec(memory_space=pltpu.HBM),
        out_shape=jax.ShapeDtypeStruct((width, 8 * units), jnp.bfloat16),
        scratch_shapes=[
            pltpu.VMEM((8 * units, width), jnp.bfloat16),
            pltpu.VMEM((width, 8 * units), jnp.bfloat16),
            pltpu.SemaphoreType.DMA((n,)),
            pltpu.SemaphoreType.DMA((len(PARTS),)),
        ],
        compiler_params=pltpu.CompilerParams(vmem_limit_bytes=24 * MB),
        cost_estimate=pl.CostEstimate(flops=0, bytes_accessed=32 * units * width, transcendentals=0),
        name="assemble",
    )(where, *(array for array, _, _ in found))


def body(weights, momentum, table, token_ids, cotangent):
    island, fsdp = lax.axis_index("island"), lax.axis_index("fsdp")
    width, hidden_units = weights.shape
    steps, tokens = token_ids.shape[1:]
    rows = table.shape[0]
    units = hidden_units // 8
    where = scalars(island, fsdp, units, rows)

    def exchange(k):
        return over_island(m[k], MASKS[0][k], MASKS[1][k])

    z = over_z(table)
    x1 = over_x(table, True)
    table_o = over_core(table)
    m = turn_cotangent(where, cotangent[0], token_ids[0])
    x1, table_o, *m = together(x1, table_o, *m)

    x2 = over_x(pack(where, [(table, ODD_ROWS, rows // 2), (x1, ODD_ROWS, rows // 2)]), False)
    k1, k2, k3 = exchange(1), exchange(2), exchange(3)
    w, mom = own_rows(where, weights, momentum, [x1])
    z, x2, k1, k2, k3, w, mom, *m[4:] = together(z, x2, k1, k2, k3, w, mom, *m[4:])

    x1z, k4, k5, z_o, x1_o = over_x(z, True), exchange(4), exchange(5), over_core(z), over_core(x1)
    cots = [add_by_row([m[0], k1, k2, k3], rows, steps)]
    x1z, k4, k5, z_o, x1_o, c0, c1, *m[6:] = together(x1z, k4, k5, z_o, x1_o, *cots[0], *m[6:])
    cots[0] = (c0, c1)

    x2z = over_x(pack(where, [(z, None, rows), (x1z, None, rows)]), False)
    y2, k6, k7, x2_o = over_y(x2, True), exchange(6), exchange(7), over_core(x2)
    cots.append(add_by_row([k4, k5], rows, steps))
    x2z, y2, k6, k7, x2_o, c0, c1 = together(x2z, y2, k6, k7, x2_o, *cots[1])
    cots[1] = (c0, c1)

    x2z_o, y2_o, x1z_o = over_core(x2z), over_core(y2), over_core(x1z)
    cots.append(add_by_row([k6, k7], rows, steps))
    pieces = [table, x1, x2, y2, z, x1z, x2z, table_o, x1_o, x2_o, y2_o, z_o, x1z_o, x2z_o]
    new = main_steps(pieces, where, w, mom, cots, tokens)
    return assemble(spread(new), where, units, width)


def solution(mesh):
    placed = (
        P(None, "fsdp"),
        P(None, "fsdp"),
        P(None, "fsdp"),
        P("island", None, None),
        P("island", None, None, "fsdp"),
    )
    return jax.shard_map(body, mesh=mesh, in_specs=placed, out_specs=P(None, "fsdp"), check_vma=False)
```

```python
import math

import jax
import jax.numpy as jnp
from jax import lax
from jax.experimental import pallas as pl
from jax.experimental.pallas import tpu as pltpu
from jax.sharding import PartitionSpec as P

beta_one = 0.9
beta_two = 0.95
adam_eps = 0.0001
inner_rate = 0.1
decay_rate = 0.1
outer_rate = 0.7
outer_moment = 0.9

MB = 1 << 20
AXES = ("island", "fsdp")
XA, XB = 1, 3
MASKS = ((0, 5, 1, 6, 4, 2, 7, 3), (0, 7, 3, 6, 4, 2, 5, 1))
PARTS = ((0, 1408), (1408, 1408), (2816, 1280))
TURNS = ((0, 768), (768, 640), (1408, 768), (2176, 640), (2816, 640), (3456, 640))
LINKS = (1, 3, 4)
VMEM_ALL = 64 * MB - 256 * 1024
IDS = 16


X, CORE, ZHI, LOW, SHIFT, PARTNERS, ISLANDS = 0, 1, 2, 3, 4, 5, 13


def scalars(island, fsdp, units):
    masks = jnp.where(fsdp % 2 == 0, jnp.asarray(MASKS[0]), jnp.asarray(MASKS[1]))
    low = jnp.minimum(island * units // 128, 8 * units // 128 - 2) * 128
    single = [(fsdp // 2) % 4, fsdp % 2, fsdp // 8, low, island * units - low]
    return jnp.concatenate(
        [jnp.stack([jnp.asarray(v, jnp.int32) for v in single]), (island ^ masks) * units, (island ^ jnp.arange(8)) * units]
    ).astype(jnp.int32)


def small():
    return pl.CostEstimate(flops=0, bytes_accessed=1024, transcendentals=0)


def swap(a, partner):
    pairs = []
    for zlo in range(2):
        for y in range(4):
            for zhi in range(2):
                for x in range(4):
                    for c in range(2):
                        px, py, pz, pc = partner(x, y, zhi * 2 + zlo, c)
                        me = (zlo * 4 + y) * 16 + zhi * 8 + x * 2 + c
                        to = ((pz % 2) * 4 + py) * 16 + (pz // 2) * 8 + px * 2 + pc
                        pairs.append((me, to))
    return lax.ppermute(a, AXES, pairs)


def over_x(a, first):
    return swap(a, lambda x, y, z, c: (x ^ (XA if (c == 0) == first else XB), y, z, c))


def over_z(a):
    return swap(a, lambda x, y, z, c: (x, y, z ^ 3, c))


def over_core(a):
    return swap(a, lambda x, y, z, c: (x, y, z, c ^ 1))


def over_island(a, mask, other=None):
    masks = (mask, mask if other is None else other)
    return swap(a, lambda x, y, z, c: (x, y ^ (masks[c] & 3), z ^ (masks[c] >> 2), c))


def slope(product, scale, factor):
    half = product * (0.5 * scale)
    bent = jnp.tanh(half)
    return (bent * (0.5 * factor) + 0.5 * factor) * (1.0 + half * (1.0 - bent))


def turn_cotangent(where, cot, ids):
    steps, tokens, hidden_units = cot.shape
    units = hidden_units // 8
    n = 8

    def kernel(where_ref, cot_ref, ids_ref, *refs):
        outs, held, turned, digits, in_sems, out_sems = refs[:n], *refs[n:]
        loads = []
        for s in range(steps):
            load = pltpu.make_async_copy(cot_ref.at[s], held.at[s], in_sems.at[s])
            load.start()
            loads.append(load)
        row = lax.broadcasted_iota(jnp.int32, (IDS, tokens), 0)
        rows = jnp.zeros((IDS, tokens), jnp.int32)
        for s in range(steps):
            one = ids_ref[s : s + 1, :]
            rows = jnp.where(row == 2 * s, one >> 8, jnp.where(row == 2 * s + 1, one & 255, rows))
        digits[...] = rows.astype(jnp.float32).astype(jnp.bfloat16)
        stores = []

        def store(source, target):
            copy = pltpu.make_async_copy(source, target, out_sems.at[len(stores)])
            copy.start()
            stores.append(copy)

        for m in range(n):
            store(digits, outs[m].at[pl.ds(steps * units, IDS), :])
        for s in range(steps):
            loads[s].wait()
            for col in range(0, hidden_units, 128):
                turned[s, col : col + 128, :] = held[s, :, col : col + 128].T
            for m in range(n):
                at = pl.multiple_of(where_ref[PARTNERS + m], 16)
                store(turned.at[s, pl.ds(at, units), :], outs[m].at[pl.ds(s * units, units), :])
        for copy in stores:
            copy.wait()

    return pl.pallas_call(
        kernel,
        in_specs=[
            pl.BlockSpec(memory_space=pltpu.SMEM),
            pl.BlockSpec(memory_space=pltpu.HBM),
            pl.BlockSpec(memory_space=pltpu.VMEM),
        ],
        out_specs=[pl.BlockSpec(memory_space=pltpu.HBM)] * n,
        out_shape=[jax.ShapeDtypeStruct((steps * units + IDS, tokens), cot.dtype)] * n,
        scratch_shapes=[
            pltpu.VMEM((steps, tokens, hidden_units), cot.dtype),
            pltpu.VMEM((steps, hidden_units, tokens), cot.dtype),
            pltpu.VMEM((IDS, tokens), cot.dtype),
            pltpu.SemaphoreType.DMA((steps,)),
            pltpu.SemaphoreType.DMA((n * (steps + 1),)),
        ],
        compiler_params=pltpu.CompilerParams(vmem_limit_bytes=VMEM_ALL),
        cost_estimate=small(),
        name="turn_cotangent",
    )(where, cot, ids)


def own_rows(where, weights, momentum, after):
    width, hidden_units = weights.shape
    units = hidden_units // 8

    def kernel(where_ref, w_ref, m_ref, _, w_out, m_out, held, turned, sems):
        stores = []
        cols = pl.ds(pl.multiple_of(where_ref[LOW], 128), 256)
        rows = pl.ds(pl.multiple_of(where_ref[SHIFT], 16), units)
        loads = []
        for k, ref in enumerate((w_ref, m_ref)):
            load = pltpu.make_async_copy(ref.at[:, cols], held.at[k], sems.at[k])
            load.start()
            loads.append(load)
        for k, out in enumerate((w_out, m_out)):
            loads[k].wait()
            for at in range(0, width, 512):
                turned[k, :, at : at + 512] = held[k, at : at + 512, :].T
            store = pltpu.make_async_copy(turned.at[k, rows, :], out, sems.at[2 + k])
            store.start()
            stores.append(store)
        for store in stores:
            store.wait()

    return pl.pallas_call(
        kernel,
        in_specs=[pl.BlockSpec(memory_space=pltpu.SMEM)] + [pl.BlockSpec(memory_space=pltpu.HBM)] * 3,
        out_specs=[pl.BlockSpec(memory_space=pltpu.HBM)] * 2,
        out_shape=[jax.ShapeDtypeStruct((units, width), weights.dtype)] * 2,
        scratch_shapes=[
            pltpu.VMEM((2, width, 256), weights.dtype),
            pltpu.VMEM((2, 256, width), weights.dtype),
            pltpu.SemaphoreType.DMA((4,)),
        ],
        compiler_params=pltpu.CompilerParams(vmem_limit_bytes=VMEM_ALL),
        cost_estimate=small(),
        name="own_rows",
    )(where, weights, momentum, *after)


def add_by_row(arrived, rows, steps):
    n = len(arrived)
    tokens = arrived[0].shape[1]
    units = (arrived[0].shape[0] - IDS) // steps
    highs = rows // 256

    def kernel(*refs):
        sources, targets, messages, sums, in_sems, out_sems = refs[:n], refs[n : n + steps], *refs[n + steps :]
        loads = [pltpu.make_async_copy(sources[m], messages.at[m], in_sems.at[m]) for m in range(n)]
        for load in loads:
            load.start()
        stores = []
        row = lax.broadcasted_iota(jnp.int32, (256, tokens), 0).astype(jnp.float32)
        for m in range(n):
            loads[m].wait()
            digits = messages[m, steps * units : steps * units + IDS, :].astype(jnp.float32)
            for step in range(steps):
                high, low = digits[2 * step : 2 * step + 1], digits[2 * step + 1 : 2 * step + 2]
                hot = jnp.where(low == row, 1.0, 0.0).astype(jnp.bfloat16)
                cot = messages[m, step * units : (step + 1) * units, :]
                parted = [cot * jnp.where(high == float(k), 1.0, 0.0).astype(jnp.bfloat16) for k in range(highs)]
                total = lax.dot_general(
                    jnp.concatenate(parted), hot, (((1,), (1,)), ((), ())), preferred_element_type=jnp.float32
                ).astype(jnp.bfloat16)
                for k in range(highs):
                    sums[m, step, :, k * 256 : (k + 1) * 256] = total[k * units : (k + 1) * units]
                store = pltpu.make_async_copy(
                    sums.at[m, step], targets[step].at[pl.ds(m * units, units), :], out_sems.at[m * steps + step]
                )
                store.start()
                stores.append(store)
        for store in stores:
            store.wait()

    return pl.pallas_call(
        kernel,
        in_specs=[pl.BlockSpec(memory_space=pltpu.HBM)] * n,
        out_specs=[pl.BlockSpec(memory_space=pltpu.HBM)] * steps,
        out_shape=[jax.ShapeDtypeStruct((n * units, rows), jnp.bfloat16)] * steps,
        scratch_shapes=[
            pltpu.VMEM((n, *arrived[0].shape), jnp.bfloat16),
            pltpu.VMEM((n, steps, units, rows), jnp.bfloat16),
            pltpu.SemaphoreType.DMA((n,)),
            pltpu.SemaphoreType.DMA((n * steps,)),
        ],
        compiler_params=pltpu.CompilerParams(vmem_limit_bytes=VMEM_ALL),
        cost_estimate=pl.CostEstimate(flops=n * 10**9, bytes_accessed=n * MB, transcendentals=0),
        name="add_by_row",
    )(*arrived)


def together(*arrays):
    n = len(arrays)
    return pl.pallas_call(
        lambda *refs: None,
        in_specs=[pl.BlockSpec(memory_space=pltpu.HBM)] * n,
        out_specs=[pl.BlockSpec(memory_space=pltpu.HBM)] * n,
        out_shape=[jax.ShapeDtypeStruct(a.shape, a.dtype) for a in arrays],
        input_output_aliases={k: k for k in range(n)},
        compiler_params=pltpu.CompilerParams(vmem_limit_bytes=VMEM_ALL),
        cost_estimate=small(),
        name="together",
    )(*arrays)


def pack(arrays):
    n, (count, width) = len(arrays), arrays[0].shape

    def kernel(*refs):
        sources, out, held, in_sems, out_sems = refs[:n], *refs[n:]
        loads, stores = [], []
        for k in range(n):
            loads.append(pltpu.make_async_copy(sources[k], held.at[k], in_sems.at[k]))
            stores.append(pltpu.make_async_copy(held.at[k], out.at[pl.ds(k * count, count), :], out_sems.at[k]))
            loads[k].start()
        for load, store in zip(loads, stores):
            load.wait()
            store.start()
        for store in stores:
            store.wait()

    return pl.pallas_call(
        kernel,
        in_specs=[pl.BlockSpec(memory_space=pltpu.HBM)] * n,
        out_specs=pl.BlockSpec(memory_space=pltpu.HBM),
        out_shape=jax.ShapeDtypeStruct((n * count, width), arrays[0].dtype),
        scratch_shapes=[
            pltpu.VMEM((n, count, width), arrays[0].dtype),
            pltpu.SemaphoreType.DMA((n,)),
            pltpu.SemaphoreType.DMA((n,)),
        ],
        compiler_params=pltpu.CompilerParams(vmem_limit_bytes=VMEM_ALL),
        cost_estimate=small(),
        name="pack",
    )(*arrays)


def places(rows, x, core, zhi):
    found = []
    for q in range(2):
        cc = core ^ q
        d1 = XA + (XB - XA) * cc
        order = ((x, 0), (x ^ d1, 0), (x ^ d1 ^ 2, 0), (x, 1), (x ^ 2, 0), (x ^ d1, 1), (x ^ d1 ^ 2, 1), (x ^ 2, 1))
        for k, (xx, zz) in enumerate(order):
            piece, first = (k, 0) if q == 0 else ((8, 0), (9, 0), (8, 1), (8, 2), (10, 0), (10, 1), (11, 0), (12, 0))[k]
            found.append((piece, first * rows, 256 * ((zhi ^ zz) * 8 + xx * 2 + cc)))
    return found


def main_steps(pieces, position, w, momentum, cots, tokens):
    rows = cots[0][0].shape[1]
    units, width = w.shape
    many = 8 * units
    scale = 1.0 / math.sqrt(width)
    first_0 = beta_one * (1.0 - beta_one) / (1.0 - beta_one**2)
    first_1 = (1.0 - beta_one) / (1.0 - beta_one**2)
    root_0 = math.sqrt(beta_two * (1.0 - beta_two) / (1.0 - beta_two**2))
    root_1 = math.sqrt((1.0 - beta_two) / (1.0 - beta_two**2))
    weight_0, weight_1 = first_0 / root_0, first_1 / root_1
    eps = adam_eps / scale
    narrow = jnp.bfloat16
    half = (slice(0, many // 2), slice(many // 2, many))
    keep = 1.0 - inner_rate * decay_rate
    block = 1024
    n, sets = len(pieces), len(cots)

    def kernel(where_ref, *refs):
        piece_refs, (w_hbm, mom_hbm), refs = refs[:n], refs[n : n + 2], refs[n + 2 :]
        cot_hbm, out_ref, refs = refs[: 2 * sets], refs[2 * sets], refs[2 * sets + 1 :]
        table, work, grads, up, cot, ratio, hidden, w_ref, mom_ref, sems, more = refs
        flat = places(rows, *(where_ref[k] for k in (X, CORE, ZHI)))
        columns = [pl.multiple_of(col, 256) for _, _, col in flat]

        def start(source, target, sem):
            copy = pltpu.make_async_copy(source, target, sem)
            copy.start()
            return copy

        def load_cots(step):
            loads, at = [], 0
            for k in range(sets):
                size = cots[k][step].shape[0]
                loads.append(start(cot_hbm[2 * k + step], cot.at[pl.ds(at, size), :], more.at[2 + k]))
                at += size
            return loads

        load_w = start(w_hbm, w_ref, more.at[0])
        copies = []
        for k, (piece, first, _) in enumerate(flat):
            copies.append(
                start(piece_refs[piece].at[pl.ds(first, rows), :], table.at[:, pl.ds(columns[k], 256)], sems.at[k])
            )
            if k == 8:
                load_c = load_cots(0)
                load_m = start(mom_hbm, mom_ref, more.at[1])
        load_w.wait()
        for k in range(16):
            copies[k].wait()
            cols = pl.ds(columns[k], 256)
            part = lax.dot_general(
                w_ref[:, cols], table[:, cols], (((1,), (1,)), ((), ())), preferred_element_type=jnp.float32
            )
            if k == 0:
                hidden[...] = part
            else:
                hidden[...] += part
        for load in load_c:
            load.wait()
        for at in range(0, rows, block):
            cols = slice(at, at + block)
            factor = slope(hidden[:, cols], scale, root_0 / tokens)
            for m in range(8):
                span = slice(m * units, (m + 1) * units)
                up[span, cols] = (cot[span, cols].astype(jnp.float32) * factor).astype(jnp.bfloat16)
        load_c = load_cots(1)

        @pl.loop(0, width // block)
        def _(i):
            cols = pl.ds(pl.multiple_of(i * block, block), block)
            halves = [jnp.dot(up[at, :], table[:, cols], preferred_element_type=jnp.float32) for at in half]
            kept = w_ref[:, cols].astype(jnp.float32) * keep
            total = jnp.zeros(kept.shape, jnp.float32)
            for m in range(8):
                span = slice(m * units, (m + 1) * units)
                g = halves[m // 4][m % 4 * units : (m % 4 + 1) * units]
                r = g * pl.reciprocal(jnp.abs(g) + eps * root_0, approx=True)
                total = total + r
                work[span, cols] = (kept - inner_rate * r).astype(jnp.bfloat16)
                grads[span, cols] = g.astype(jnp.bfloat16)
            ratio[:, cols] = total

        for load in load_c:
            load.wait()

        @pl.loop(0, rows // block)
        def _(t):
            at = pl.ds(pl.multiple_of(t * block, block), block)
            products = [
                lax.dot_general(
                    work[rows_of, :], table[at, :], (((1,), (1,)), ((), ())), preferred_element_type=jnp.float32
                )
                for rows_of in half
            ]
            for rows_of, product in zip(half, products):
                up[rows_of, at] = (cot[rows_of, at].astype(jnp.float32) * slope(product, scale, root_1 / tokens)).astype(
                    jnp.bfloat16
                )

        load_m.wait()

        @pl.loop(0, width // block)
        def _(i):
            cols = pl.ds(pl.multiple_of(i * block, block), block)
            halves = [jnp.dot(up[at, :], table[:, cols], preferred_element_type=jnp.float32) for at in half]
            start_w = w_ref[:, cols].astype(jnp.float32)
            total = jnp.zeros(start_w.shape, jnp.float32)
            for m in range(8):
                span = slice(m * units, (m + 1) * units)
                b = halves[m // 4][m % 4 * units : (m % 4 + 1) * units].astype(narrow)
                a = grads[span, cols]
                v = a * a + b * b + narrow(1e-30)
                r = (a + narrow(weight_1 / weight_0) * b) * pl.reciprocal(
                    v * lax.rsqrt(v) + narrow(eps), approx=True
                )
                total = total + r.astype(jnp.float32)
            mean = (1.0 - keep * keep) * start_w + (inner_rate / 8.0) * (keep * ratio[:, cols] + weight_0 * total)
            moment = outer_moment * mom_ref[:, cols].astype(jnp.float32) + mean
            out_ref[:, cols] = (start_w - outer_rate * (mean + outer_moment * moment)).astype(jnp.bfloat16)

    return pl.pallas_call(
        kernel,
        in_specs=[pl.BlockSpec(memory_space=pltpu.SMEM)] + [pl.BlockSpec(memory_space=pltpu.HBM)] * (n + 2 + 2 * sets),
        out_specs=pl.BlockSpec(memory_space=pltpu.VMEM),
        out_shape=jax.ShapeDtypeStruct((units, width), jnp.bfloat16),
        scratch_shapes=[
            pltpu.VMEM((rows, width), jnp.bfloat16),
            pltpu.VMEM((many, width), jnp.bfloat16),
            pltpu.VMEM((many, width), jnp.bfloat16),
            pltpu.VMEM((many, rows), jnp.bfloat16),
            pltpu.VMEM((many, rows), jnp.bfloat16),
            pltpu.VMEM((units, width), jnp.float32),
            pltpu.VMEM((units, rows), jnp.float32),
            pltpu.VMEM((units, width), jnp.bfloat16),
            pltpu.VMEM((units, width), jnp.bfloat16),
            pltpu.SemaphoreType.DMA((16,)),
            pltpu.SemaphoreType.DMA((2 + sets,)),
        ],
        compiler_params=pltpu.CompilerParams(vmem_limit_bytes=VMEM_ALL),
        cost_estimate=pl.CostEstimate(flops=52 * units * rows * width, bytes_accessed=rows * width * 2, transcendentals=0),
        name="main_steps",
    )(position, *pieces, w, momentum, *(c for pair in cots for c in pair))


def spread(new):
    e1, e2, e3 = LINKS
    near = [over_island(new, e) for e in LINKS]
    far = [over_island(near[1], e1), over_island(near[2], e2), over_island(near[0], e3)]
    found = [(new, 0, 0), (near[0], 0, e1), (near[1], 0, e2), (near[2], 0, e3)]
    found += [(far[0], 0, e1 ^ e2), (far[1], 0, e2 ^ e3), (far[2], 0, e1 ^ e3)]
    for (low, size), source, e in zip(PARTS, (far[1], far[2], far[0]), LINKS):
        found.append((over_island(source[:, low : low + size], e), low, e1 ^ e2 ^ e3))
    return found


def assemble(found, where, units, width):
    n = len(found)

    def kernel(where_ref, *refs):
        arrays, out, held, turned, sems, out_sems = refs[:n], refs[n], refs[n + 1], refs[n + 2], refs[n + 3], refs[n + 4]
        waits = [[] for _ in TURNS]
        for p, (low, length) in enumerate(TURNS):
            for k, (array, first, mask) in enumerate(found):
                if first <= low < first + array.shape[1]:
                    row = pl.multiple_of(where_ref[ISLANDS + mask], 16)
                    copy = pltpu.make_async_copy(
                        arrays[k].at[:, pl.ds(low - first, length)],
                        held.at[pl.ds(row, units), pl.ds(low, length)],
                        sems.at[p, len(waits[p])],
                    )
                    copy.start()
                    waits[p].append(copy)
        outs = []
        for p, (low, length) in enumerate(TURNS):
            for copy in waits[p]:
                copy.wait()
            for col in range(low, low + length, 128):
                turned[col : col + 128, :] = held[:, col : col + 128].T
            copy = pltpu.make_async_copy(
                turned.at[pl.ds(low, length), :], out.at[pl.ds(low, length), :], out_sems.at[p]
            )
            copy.start()
            outs.append(copy)
        for copy in outs:
            copy.wait()

    return pl.pallas_call(
        kernel,
        in_specs=[pl.BlockSpec(memory_space=pltpu.SMEM)] + [pl.BlockSpec(memory_space=pltpu.HBM)] * n,
        out_specs=pl.BlockSpec(memory_space=pltpu.HBM),
        out_shape=jax.ShapeDtypeStruct((width, 8 * units), jnp.bfloat16),
        scratch_shapes=[
            pltpu.VMEM((8 * units, width), jnp.bfloat16),
            pltpu.VMEM((width, 8 * units), jnp.bfloat16),
            pltpu.SemaphoreType.DMA((len(TURNS), 8)),
            pltpu.SemaphoreType.DMA((len(TURNS),)),
        ],
        compiler_params=pltpu.CompilerParams(vmem_limit_bytes=24 * MB),
        cost_estimate=pl.CostEstimate(flops=0, bytes_accessed=32 * units * width, transcendentals=0),
        name="assemble",
    )(where, *(array for array, _, _ in found))


def body(weights, momentum, table, token_ids, cotangent):
    island, fsdp = lax.axis_index("island"), lax.axis_index("fsdp")
    width, hidden_units = weights.shape
    steps, tokens = token_ids.shape[1:]
    rows = table.shape[0]
    units = hidden_units // 8
    where = scalars(island, fsdp, units)

    def exchange(k):
        return over_island(m[k], MASKS[0][k], MASKS[1][k])

    z, x1, x2 = over_z(table), over_x(table, True), over_x(table, False)
    m = list(turn_cotangent(where, cotangent[0], token_ids[0]))
    w, mom = own_rows(where, weights, momentum, m[:1])
    k1, k2 = exchange(1), exchange(2)
    z, x1, x2, k1, k2, w, mom, *m[3:] = together(z, x1, x2, k1, k2, w, mom, *m[3:])

    x1z, x3, x2z, k3 = over_z(x1), over_x(x1, False), over_x(z, False), exchange(3)
    x1_o = over_core(x1)
    c0, c1 = add_by_row([m[0], k1, k2], rows, steps)
    k3, x1_o, m[4], m[5] = together(k3, x1_o, m[4], m[5])
    k4, k5 = exchange(4), exchange(5)
    early = pack([table, x2, z])
    x1z, x3, x2z, k4, k5, early, c0, c1, *m[6:] = together(x1z, x3, x2z, k4, k5, early, c0, c1, *m[6:])
    cots = [(c0, c1)]

    x3z, k6, k7, early_o = over_x(x1z, False), exchange(6), exchange(7), over_core(early)
    late_o = over_core(pack([x3, x1z]))
    c0, c1 = add_by_row([k3, k4, k5], rows, steps)
    x3z, k6, k7, early_o, late_o, c0, c1 = together(x3z, k6, k7, early_o, late_o, c0, c1)
    cots.append((c0, c1))

    others = [early_o, x1_o, late_o, over_core(x2z), over_core(x3z)]
    cots.append(add_by_row([k6, k7], rows, steps))
    pieces = [table, x1, x2, z, x3, x1z, x2z, x3z, *others]
    new = main_steps(pieces, where, w, mom, cots, tokens)
    return assemble(spread(new), where, units, width)


def solution(mesh):
    placed = (
        P(None, "fsdp"),
        P(None, "fsdp"),
        P(None, "fsdp"),
        P("island", None, None),
        P("island", None, None, "fsdp"),
    )
    return jax.shard_map(body, mesh=mesh, in_specs=placed, out_specs=P(None, "fsdp"), check_vma=False)
```

```python
import math

import jax
import jax.numpy as jnp
from jax import lax
from jax.experimental import pallas as pl
from jax.experimental.pallas import tpu as pltpu
from jax.sharding import PartitionSpec as P

beta_one = 0.9
beta_two = 0.95
adam_eps = 0.0001
inner_rate = 0.1
decay_rate = 0.1
outer_rate = 0.7
outer_moment = 0.9

MB = 1 << 20
AXES = ("island", "fsdp")
XA, XB = 1, 3
MASKS = ((0, 5, 1, 6, 4, 2, 7, 3), (0, 7, 3, 6, 4, 2, 5, 1))
PARTS = ((0, 1408), (1408, 1408), (2816, 1280))
TURNS = ((0, 768), (768, 640), (1408, 768), (2176, 640), (2816, 640), (3456, 640))
LAST = 6
LINKS = (1, 3, 4)
VMEM_ALL = 64 * MB - 256 * 1024
IDS = 16


def row_of(where_ref, mask, units):
    return pl.multiple_of((where_ref[0] ^ mask) * units, 16)


def window_of(where_ref, mask, units):
    first = (where_ref[0] ^ mask) * units
    low = jnp.minimum(first >> 7, 8 * units // 128 - 2) * 128
    return pl.multiple_of(low, 128), pl.multiple_of(first - low, 16)


def small():
    return pl.CostEstimate(flops=0, bytes_accessed=1024, transcendentals=0)


def swap(a, partner):
    pairs = []
    for zlo in range(2):
        for y in range(4):
            for zhi in range(2):
                for x in range(4):
                    for c in range(2):
                        px, py, pz, pc = partner(x, y, zhi * 2 + zlo, c)
                        me = (zlo * 4 + y) * 16 + zhi * 8 + x * 2 + c
                        to = ((pz % 2) * 4 + py) * 16 + (pz // 2) * 8 + px * 2 + pc
                        pairs.append((me, to))
    return lax.ppermute(a, AXES, pairs)


def over_x(a, first):
    return swap(a, lambda x, y, z, c: (x ^ (XA if (c == 0) == first else XB), y, z, c))


def over_z(a):
    return swap(a, lambda x, y, z, c: (x, y, z ^ 3, c))


def over_core(a):
    return swap(a, lambda x, y, z, c: (x, y, z, c ^ 1))


def over_island(a, mask, other=None):
    masks = (mask, mask if other is None else other)
    return swap(a, lambda x, y, z, c: (x, y ^ (masks[c] & 3), z ^ (masks[c] >> 2), c))


def slope(product, scale, factor):
    half = product * (0.5 * scale)
    bent = jnp.tanh(half)
    return (bent * (0.5 * factor) + 0.5 * factor) * (1.0 + half * (1.0 - bent))


def turn_cotangent(where, cot, ids):
    steps, tokens, hidden_units = cot.shape
    units = hidden_units // 8
    n = 8

    def kernel(where_ref, cot_ref, ids_ref, *refs):
        outs, held, turned, digits, in_sems, out_sems = refs[:n], *refs[n:]
        loads = []
        for s in range(steps):
            load = pltpu.make_async_copy(cot_ref.at[s], held.at[s], in_sems.at[s])
            load.start()
            loads.append(load)
        row = lax.broadcasted_iota(jnp.int32, (IDS, tokens), 0)
        rows = jnp.zeros((IDS, tokens), jnp.int32)
        for s in range(steps):
            one = ids_ref[s : s + 1, :]
            rows = jnp.where(row == 2 * s, one >> 8, jnp.where(row == 2 * s + 1, one & 255, rows))
        digits[...] = rows.astype(jnp.float32).astype(jnp.bfloat16)
        stores = []

        def store(source, target):
            copy = pltpu.make_async_copy(source, target, out_sems.at[len(stores)])
            copy.start()
            stores.append(copy)

        for m in range(n):
            store(digits, outs[m].at[pl.ds(steps * units, IDS), :])
        for s in range(steps):
            loads[s].wait()
            for col in range(0, hidden_units, 128):
                turned[s, col : col + 128, :] = held[s, :, col : col + 128].T
            for m in range(n):
                at = row_of(where_ref, jnp.where((where_ref[1] & 1) == 0, MASKS[0][m], MASKS[1][m]), units)
                store(turned.at[s, pl.ds(at, units), :], outs[m].at[pl.ds(s * units, units), :])
        for copy in stores:
            copy.wait()

    return pl.pallas_call(
        kernel,
        in_specs=[
            pl.BlockSpec(memory_space=pltpu.SMEM),
            pl.BlockSpec(memory_space=pltpu.HBM),
            pl.BlockSpec(memory_space=pltpu.VMEM),
        ],
        out_specs=[pl.BlockSpec(memory_space=pltpu.HBM)] * n,
        out_shape=[jax.ShapeDtypeStruct((steps * units + IDS, tokens), cot.dtype)] * n,
        scratch_shapes=[
            pltpu.VMEM((steps, tokens, hidden_units), cot.dtype),
            pltpu.VMEM((steps, hidden_units, tokens), cot.dtype),
            pltpu.VMEM((IDS, tokens), cot.dtype),
            pltpu.SemaphoreType.DMA((steps,)),
            pltpu.SemaphoreType.DMA((n * (steps + 1),)),
        ],
        compiler_params=pltpu.CompilerParams(vmem_limit_bytes=VMEM_ALL),
        cost_estimate=small(),
        name="turn_cotangent",
    )(where, cot, ids)


def own_rows(where, weights, momentum, after):
    width, hidden_units = weights.shape
    units = hidden_units // 8

    def kernel(where_ref, w_ref, m_ref, _, w_out, m_out, held, turned, sems):
        stores = []
        low, shift = window_of(where_ref, 0, units)
        cols, rows = pl.ds(low, 256), pl.ds(shift, units)
        loads = []
        for k, ref in enumerate((w_ref, m_ref)):
            load = pltpu.make_async_copy(ref.at[:, cols], held.at[k], sems.at[k])
            load.start()
            loads.append(load)
        for k, out in enumerate((w_out, m_out)):
            loads[k].wait()
            for at in range(0, width, 512):
                turned[k, :, at : at + 512] = held[k, at : at + 512, :].T
            store = pltpu.make_async_copy(turned.at[k, rows, :], out, sems.at[2 + k])
            store.start()
            stores.append(store)
        for store in stores:
            store.wait()

    return pl.pallas_call(
        kernel,
        in_specs=[pl.BlockSpec(memory_space=pltpu.SMEM)] + [pl.BlockSpec(memory_space=pltpu.HBM)] * 3,
        out_specs=[pl.BlockSpec(memory_space=pltpu.HBM)] * 2,
        out_shape=[jax.ShapeDtypeStruct((units, width), weights.dtype)] * 2,
        scratch_shapes=[
            pltpu.VMEM((2, width, 256), weights.dtype),
            pltpu.VMEM((2, 256, width), weights.dtype),
            pltpu.SemaphoreType.DMA((4,)),
        ],
        compiler_params=pltpu.CompilerParams(vmem_limit_bytes=VMEM_ALL),
        cost_estimate=small(),
        name="own_rows",
    )(where, weights, momentum, *after)


def add_by_row(arrived, rows, steps):
    n = len(arrived)
    tokens = arrived[0].shape[1]
    units = (arrived[0].shape[0] - IDS) // steps
    highs = rows // 256

    def kernel(*refs):
        sources, targets, messages, sums, in_sems, out_sems = refs[:n], refs[n : n + steps], *refs[n + steps :]
        loads = [pltpu.make_async_copy(sources[m], messages.at[m], in_sems.at[m]) for m in range(n)]
        for load in loads:
            load.start()
        stores = []
        row = lax.broadcasted_iota(jnp.int32, (256, tokens), 0).astype(jnp.float32)
        for m in range(n):
            loads[m].wait()
            digits = messages[m, steps * units : steps * units + IDS, :].astype(jnp.float32)
            for step in range(steps):
                high, low = digits[2 * step : 2 * step + 1], digits[2 * step + 1 : 2 * step + 2]
                hot = jnp.where(low == row, 1.0, 0.0).astype(jnp.bfloat16)
                cot = messages[m, step * units : (step + 1) * units, :]
                parted = [cot * jnp.where(high == float(k), 1.0, 0.0).astype(jnp.bfloat16) for k in range(highs)]
                total = lax.dot_general(
                    jnp.concatenate(parted), hot, (((1,), (1,)), ((), ())), preferred_element_type=jnp.float32
                ).astype(jnp.bfloat16)
                for k in range(highs):
                    sums[m, step, :, k * 256 : (k + 1) * 256] = total[k * units : (k + 1) * units]
                store = pltpu.make_async_copy(
                    sums.at[m, step], targets[step].at[pl.ds(m * units, units), :], out_sems.at[m * steps + step]
                )
                store.start()
                stores.append(store)
        for store in stores:
            store.wait()

    return pl.pallas_call(
        kernel,
        in_specs=[pl.BlockSpec(memory_space=pltpu.HBM)] * n,
        out_specs=[pl.BlockSpec(memory_space=pltpu.HBM)] * steps,
        out_shape=[jax.ShapeDtypeStruct((n * units, rows), jnp.bfloat16)] * steps,
        scratch_shapes=[
            pltpu.VMEM((n, *arrived[0].shape), jnp.bfloat16),
            pltpu.VMEM((n, steps, units, rows), jnp.bfloat16),
            pltpu.SemaphoreType.DMA((n,)),
            pltpu.SemaphoreType.DMA((n * steps,)),
        ],
        compiler_params=pltpu.CompilerParams(vmem_limit_bytes=VMEM_ALL),
        cost_estimate=pl.CostEstimate(flops=n * 10**9, bytes_accessed=n * MB, transcendentals=0),
        name="add_by_row",
    )(*arrived)


def together(*arrays):
    n = len(arrays)
    return pl.pallas_call(
        lambda *refs: None,
        in_specs=[pl.BlockSpec(memory_space=pltpu.HBM)] * n,
        out_specs=[pl.BlockSpec(memory_space=pltpu.HBM)] * n,
        out_shape=[jax.ShapeDtypeStruct(a.shape, a.dtype) for a in arrays],
        input_output_aliases={k: k for k in range(n)},
        compiler_params=pltpu.CompilerParams(vmem_limit_bytes=VMEM_ALL),
        cost_estimate=small(),
        name="together",
    )(*arrays)


def pack(arrays):
    n, (count, width) = len(arrays), arrays[0].shape

    def kernel(*refs):
        sources, out, held, in_sems, out_sems = refs[:n], *refs[n:]
        loads, stores = [], []
        for k in range(n):
            loads.append(pltpu.make_async_copy(sources[k], held.at[k], in_sems.at[k]))
            stores.append(pltpu.make_async_copy(held.at[k], out.at[pl.ds(k * count, count), :], out_sems.at[k]))
            loads[k].start()
        for load, store in zip(loads, stores):
            load.wait()
            store.start()
        for store in stores:
            store.wait()

    return pl.pallas_call(
        kernel,
        in_specs=[pl.BlockSpec(memory_space=pltpu.HBM)] * n,
        out_specs=pl.BlockSpec(memory_space=pltpu.HBM),
        out_shape=jax.ShapeDtypeStruct((n * count, width), arrays[0].dtype),
        scratch_shapes=[
            pltpu.VMEM((n, count, width), arrays[0].dtype),
            pltpu.SemaphoreType.DMA((n,)),
            pltpu.SemaphoreType.DMA((n,)),
        ],
        compiler_params=pltpu.CompilerParams(vmem_limit_bytes=VMEM_ALL),
        cost_estimate=small(),
        name="pack",
    )(*arrays)


def places(rows, x, core, zhi):
    found = []
    for q in range(2):
        cc = core ^ q
        d1 = XA + (XB - XA) * cc
        order = ((x, 0), (x ^ d1, 0), (x ^ d1 ^ 2, 0), (x, 1), (x ^ 2, 0), (x ^ d1, 1), (x ^ d1 ^ 2, 1), (x ^ 2, 1))
        for k, (xx, zz) in enumerate(order):
            piece, first = (k, 0) if q == 0 else ((8, 0), (9, 0), (8, 1), (8, 2), (10, 0), (10, 1), (11, 0), (12, 0))[k]
            found.append((piece, first * rows, 256 * ((zhi ^ zz) * 8 + xx * 2 + cc)))
    return found


def main_steps(pieces, position, w, momentum, cots, tokens):
    rows = cots[0][0].shape[1]
    units, width = w.shape
    many = 8 * units
    scale = 1.0 / math.sqrt(width)
    first_0 = beta_one * (1.0 - beta_one) / (1.0 - beta_one**2)
    first_1 = (1.0 - beta_one) / (1.0 - beta_one**2)
    root_0 = math.sqrt(beta_two * (1.0 - beta_two) / (1.0 - beta_two**2))
    root_1 = math.sqrt((1.0 - beta_two) / (1.0 - beta_two**2))
    weight_0, weight_1 = first_0 / root_0, first_1 / root_1
    eps = adam_eps / scale
    narrow = jnp.bfloat16
    half = (slice(0, many // 2), slice(many // 2, many))
    keep = 1.0 - inner_rate * decay_rate
    block, wide = 1024, 2048
    n, sets = len(pieces), len(cots)

    def kernel(where_ref, *refs):
        piece_refs, (w_hbm, mom_hbm), refs = refs[:n], refs[n : n + 2], refs[n + 2 :]
        cot_hbm, out_ref, refs = refs[: 2 * sets], refs[2 * sets], refs[2 * sets + 1 :]
        table, work, grads, up, cot, ratio, hidden, w_ref, mom_ref, sems, more = refs
        flat = places(rows, (where_ref[1] >> 1) & 3, where_ref[1] & 1, where_ref[1] >> 3)
        columns = [pl.multiple_of(col, 256) for _, _, col in flat]

        def start(source, target, sem):
            copy = pltpu.make_async_copy(source, target, sem)
            copy.start()
            return copy

        def load_cots(step):
            loads, at = [], 0
            for k in range(sets):
                size = cots[k][step].shape[0]
                loads.append(start(cot_hbm[2 * k + step], cot.at[pl.ds(at, size), :], more.at[2 + k]))
                at += size
            return loads

        load_w = start(w_hbm, w_ref, more.at[0])
        copies = []
        for k, (piece, first, _) in enumerate(flat):
            copies.append(
                start(piece_refs[piece].at[pl.ds(first, rows), :], table.at[:, pl.ds(columns[k], 256)], sems.at[k])
            )
            if k == 8:
                load_c = load_cots(0)
                load_m = start(mom_hbm, mom_ref, more.at[1])
        load_w.wait()
        for k in range(16):
            copies[k].wait()
            cols = pl.ds(columns[k], 256)
            part = lax.dot_general(
                w_ref[:, cols], table[:, cols], (((1,), (1,)), ((), ())), preferred_element_type=jnp.float32
            )
            if k == 0:
                hidden[...] = part
            else:
                hidden[...] += part
        for load in load_c:
            load.wait()
        for at in range(0, rows, block):
            cols = slice(at, at + block)
            factor = slope(hidden[:, cols], scale, root_0 / tokens)
            for m in range(8):
                span = slice(m * units, (m + 1) * units)
                up[span, cols] = (cot[span, cols].astype(jnp.float32) * factor).astype(jnp.bfloat16)
        load_c = load_cots(1)

        @pl.loop(0, width // wide)
        def _(i):
            cols = pl.ds(pl.multiple_of(i * wide, wide), wide)
            halves = [jnp.dot(up[at, :], table[:, cols], preferred_element_type=jnp.float32) for at in half]
            kept = w_ref[:, cols].astype(jnp.float32) * keep
            total = jnp.zeros(kept.shape, jnp.float32)
            for m in range(8):
                span = slice(m * units, (m + 1) * units)
                g = halves[m // 4][m % 4 * units : (m % 4 + 1) * units]
                r = g * pl.reciprocal(jnp.abs(g) + eps * root_0, approx=True)
                total = total + r
                work[span, cols] = (kept - inner_rate * r).astype(jnp.bfloat16)
                grads[span, cols] = g.astype(jnp.bfloat16)
            ratio[:, cols] = total

        for load in load_c:
            load.wait()

        @pl.loop(0, rows // block)
        def _(t):
            at = pl.ds(pl.multiple_of(t * block, block), block)
            products = [
                lax.dot_general(
                    work[rows_of, :], table[at, :], (((1,), (1,)), ((), ())), preferred_element_type=jnp.float32
                )
                for rows_of in half
            ]
            for rows_of, product in zip(half, products):
                up[rows_of, at] = (cot[rows_of, at].astype(jnp.float32) * slope(product, scale, root_1 / tokens)).astype(
                    jnp.bfloat16
                )

        load_m.wait()

        @pl.loop(0, width // wide)
        def _(i):
            cols = pl.ds(pl.multiple_of(i * wide, wide), wide)
            halves = [jnp.dot(up[at, :], table[:, cols], preferred_element_type=jnp.float32) for at in half]
            start_w = w_ref[:, cols].astype(jnp.float32)
            total = jnp.zeros(start_w.shape, jnp.float32)
            for m in range(8):
                span = slice(m * units, (m + 1) * units)
                b = halves[m // 4][m % 4 * units : (m % 4 + 1) * units].astype(narrow)
                a = grads[span, cols]
                v = a * a + b * b + narrow(1e-30)
                r = (a + narrow(weight_1 / weight_0) * b) * pl.reciprocal(
                    v * lax.rsqrt(v) + narrow(eps), approx=True
                )
                total = total + r.astype(jnp.float32)
            mean = (1.0 - keep * keep) * start_w + (inner_rate / 8.0) * (keep * ratio[:, cols] + weight_0 * total)
            moment = outer_moment * mom_ref[:, cols].astype(jnp.float32) + mean
            out_ref[:, cols] = (start_w - outer_rate * (mean + outer_moment * moment)).astype(jnp.bfloat16)

    return pl.pallas_call(
        kernel,
        in_specs=[pl.BlockSpec(memory_space=pltpu.SMEM)] + [pl.BlockSpec(memory_space=pltpu.HBM)] * (n + 2 + 2 * sets),
        out_specs=pl.BlockSpec(memory_space=pltpu.VMEM),
        out_shape=jax.ShapeDtypeStruct((units, width), jnp.bfloat16),
        scratch_shapes=[
            pltpu.VMEM((rows, width), jnp.bfloat16),
            pltpu.VMEM((many, width), jnp.bfloat16),
            pltpu.VMEM((many, width), jnp.bfloat16),
            pltpu.VMEM((many, rows), jnp.bfloat16),
            pltpu.VMEM((many, rows), jnp.bfloat16),
            pltpu.VMEM((units, width), jnp.float32),
            pltpu.VMEM((units, rows), jnp.float32),
            pltpu.VMEM((units, width), jnp.bfloat16),
            pltpu.VMEM((units, width), jnp.bfloat16),
            pltpu.SemaphoreType.DMA((16,)),
            pltpu.SemaphoreType.DMA((2 + sets,)),
        ],
        compiler_params=pltpu.CompilerParams(vmem_limit_bytes=VMEM_ALL),
        cost_estimate=pl.CostEstimate(flops=52 * units * rows * width, bytes_accessed=rows * width * 2, transcendentals=0),
        name="main_steps",
    )(position, *pieces, w, momentum, *(c for pair in cots for c in pair))


def spread(new):
    e1, e2, e3 = LINKS
    near = [over_island(new, e) for e in LINKS]
    far = [over_island(near[1], e1), over_island(near[2], e2), over_island(near[0], e3)]
    found = [(new, 0), (near[0], e1), (near[1], e2), (near[2], e3)]
    found += [(far[0], e1 ^ e2), (far[1], e2 ^ e3), (far[2], e1 ^ e3)]
    last = []
    for (low, size), source, e in zip(PARTS, (far[1], far[2], far[0]), LINKS):
        last.append((over_island(source[:, low : low + size], e), low))
    return found, last


def assemble(found, where, units, width):
    n = len(found)

    def kernel(where_ref, *refs):
        arrays, out, held, turned, sems, out_sems = refs[:n], *refs[n:]
        waits = []
        for p, (low, length) in enumerate(TURNS):
            copies = []
            for k, (_, mask) in enumerate(found):
                row = row_of(where_ref, mask, units)
                part = pl.ds(low, length)
                copy = pltpu.make_async_copy(
                    arrays[k].at[:, part], held.at[pl.ds(row, units), part], sems.at[p, k]
                )
                copy.start()
                copies.append(copy)
            waits.append(copies)
        row = row_of(where_ref, LAST, units)
        held[pl.ds(row, units), :] = jnp.zeros((units, width), held.dtype)
        outs = []
        for p, (low, length) in enumerate(TURNS):
            for copy in waits[p]:
                copy.wait()
            for col in range(low, low + length, 128):
                turned[col : col + 128, :] = held[:, col : col + 128].T
            copy = pltpu.make_async_copy(
                turned.at[pl.ds(low, length), :], out.at[pl.ds(low, length), :], out_sems.at[p]
            )
            copy.start()
            outs.append(copy)
        for copy in outs:
            copy.wait()

    return pl.pallas_call(
        kernel,
        in_specs=[pl.BlockSpec(memory_space=pltpu.SMEM)] + [pl.BlockSpec(memory_space=pl.ANY)] * n,
        out_specs=pl.BlockSpec(memory_space=pltpu.HBM),
        out_shape=jax.ShapeDtypeStruct((width, 8 * units), jnp.bfloat16),
        scratch_shapes=[
            pltpu.VMEM((8 * units, width), jnp.bfloat16),
            pltpu.VMEM((width, 8 * units), jnp.bfloat16),
            pltpu.SemaphoreType.DMA((len(TURNS), n)),
            pltpu.SemaphoreType.DMA((len(TURNS),)),
        ],
        compiler_params=pltpu.CompilerParams(vmem_limit_bytes=24 * MB),
        cost_estimate=pl.CostEstimate(flops=0, bytes_accessed=32 * units * width, transcendentals=0),
        name="assemble",
    )(where, *(array for array, _ in found))


def complete(whole, last, where, units, width):
    n = len(last)
    window = 256

    def kernel(where_ref, whole_ref, *refs):
        arrays, out, kept, held, merged, in_sems, sems, out_sems = refs[:n], *refs[n:]
        low, shift = window_of(where_ref, LAST, units)
        cols = pl.ds(low, window)
        loads, arrivals = [], []
        for k, (array, low) in enumerate(last):
            part = pl.ds(low, array.shape[1])
            arrival = pltpu.make_async_copy(arrays[k], held.at[pl.ds(shift, units), part], sems.at[k])
            load = pltpu.make_async_copy(whole_ref.at[part, cols], kept.at[part, :], in_sems.at[k])
            arrival.start()
            load.start()
            loads.append(load)
            arrivals.append(arrival)
        lane = lax.broadcasted_iota(jnp.int32, (128, window), 1)
        ours = (lane >= shift) & (lane < shift + units)
        stores = []
        for k, (array, low) in enumerate(last):
            loads[k].wait()
            arrivals[k].wait()
            for col in range(low, low + array.shape[1], 128):
                here = slice(col, col + 128)
                merged[here, :] = jnp.where(ours, held[:, here].T.astype(jnp.float32), kept[here, :].astype(jnp.float32)).astype(
                    merged.dtype
                )
            part = pl.ds(low, array.shape[1])
            store = pltpu.make_async_copy(merged.at[part, :], out.at[part, cols], out_sems.at[k])
            store.start()
            stores.append(store)
        for store in stores:
            store.wait()

    return pl.pallas_call(
        kernel,
        in_specs=[pl.BlockSpec(memory_space=pltpu.SMEM), pl.BlockSpec(memory_space=pltpu.HBM)]
        + [pl.BlockSpec(memory_space=pl.ANY)] * n,
        out_specs=pl.BlockSpec(memory_space=pltpu.HBM),
        out_shape=jax.ShapeDtypeStruct(whole.shape, whole.dtype),
        input_output_aliases={1: 0},
        scratch_shapes=[
            pltpu.VMEM((width, window), whole.dtype),
            pltpu.VMEM((window, width), whole.dtype),
            pltpu.VMEM((width, window), whole.dtype),
            pltpu.SemaphoreType.DMA((n,)),
            pltpu.SemaphoreType.DMA((n,)),
            pltpu.SemaphoreType.DMA((n,)),
        ],
        compiler_params=pltpu.CompilerParams(vmem_limit_bytes=16 * MB),
        cost_estimate=small(),
        name="complete",
    )(where, whole, *(array for array, _ in last))


def body(weights, momentum, table, token_ids, cotangent):
    island, fsdp = lax.axis_index("island"), lax.axis_index("fsdp")
    width, hidden_units = weights.shape
    steps, tokens = token_ids.shape[1:]
    rows = table.shape[0]
    units = hidden_units // 8
    where = jnp.stack([island, fsdp]).astype(jnp.int32)

    def exchange(k):
        return over_island(m[k], MASKS[0][k], MASKS[1][k])

    z, x1, x2 = over_z(table), over_x(table, True), over_x(table, False)
    m = list(turn_cotangent(where, cotangent[0], token_ids[0]))
    w, mom = own_rows(where, weights, momentum, m[:1])
    k1, k2 = exchange(1), exchange(2)
    z, x1, x2, k1, k2, w, mom, *m[3:] = together(z, x1, x2, k1, k2, w, mom, *m[3:])

    x1z, x3, x2z, k3 = over_z(x1), over_x(x1, False), over_x(z, False), exchange(3)
    x1_o = over_core(x1)
    c0, c1 = add_by_row([m[0], k1, k2], rows, steps)
    k3, x1_o, m[4], m[5] = together(k3, x1_o, m[4], m[5])
    k4, k5 = exchange(4), exchange(5)
    early = pack([table, x2, z])
    x1z, x3, x2z, k4, k5, early, c0, c1, *m[6:] = together(x1z, x3, x2z, k4, k5, early, c0, c1, *m[6:])
    cots = [(c0, c1)]

    x3z, k6, k7, early_o = over_x(x1z, False), exchange(6), exchange(7), over_core(early)
    late_o = over_core(pack([x3, x1z]))
    c0, c1 = add_by_row([k3, k4, k5], rows, steps)
    x3z, k6, k7, early_o, late_o, c0, c1 = together(x3z, k6, k7, early_o, late_o, c0, c1)
    cots.append((c0, c1))

    others = [early_o, x1_o, late_o, over_core(x2z), over_core(x3z)]
    cots.append(add_by_row([k6, k7], rows, steps))
    pieces = [table, x1, x2, z, x3, x1z, x2z, x3z, *others]
    new = main_steps(pieces, where, w, mom, cots, tokens)
    found, last = spread(new)
    return complete(assemble(found, where, units, width), last, where, units, width)


def solution(mesh):
    placed = (
        P(None, "fsdp"),
        P(None, "fsdp"),
        P(None, "fsdp"),
        P("island", None, None),
        P("island", None, None, "fsdp"),
    )
    return jax.shard_map(body, mesh=mesh, in_specs=placed, out_specs=P(None, "fsdp"), check_vma=False)
```

```python
import math

import jax
import jax.numpy as jnp
from jax import lax
from jax.experimental import pallas as pl
from jax.experimental.pallas import tpu as pltpu
from jax.sharding import PartitionSpec as P

beta_one = 0.9
beta_two = 0.95
adam_eps = 0.0001
inner_rate = 0.1
decay_rate = 0.1
outer_rate = 0.7
outer_moment = 0.9

MB = 1 << 20
AXES = ("island", "fsdp")
XA, XB = 1, 3
MASKS = ((0, 5, 1, 6, 4, 2, 7, 3), (0, 7, 3, 6, 4, 2, 5, 1))
PARTS = ((0, 1408), (1408, 1408), (2816, 1280))
TURNS = ((0, 768), (768, 640), (1408, 768), (2176, 640), (2816, 640), (3456, 640))
LAST = 6
LINKS = (1, 3, 4)
VMEM_ALL = 64 * MB - 256 * 1024
IDS = 16


def row_of(where_ref, mask, units):
    return pl.multiple_of((where_ref[0] ^ mask) * units, 16)


def window_of(where_ref, mask, units):
    first = (where_ref[0] ^ mask) * units
    low = jnp.minimum(first >> 7, 8 * units // 128 - 2) * 128
    return pl.multiple_of(low, 128), pl.multiple_of(first - low, 16)


def small():
    return pl.CostEstimate(flops=0, bytes_accessed=1024, transcendentals=0)


def swap(a, partner):
    pairs = []
    for zlo in range(2):
        for y in range(4):
            for zhi in range(2):
                for x in range(4):
                    for c in range(2):
                        px, py, pz, pc = partner(x, y, zhi * 2 + zlo, c)
                        me = (zlo * 4 + y) * 16 + zhi * 8 + x * 2 + c
                        to = ((pz % 2) * 4 + py) * 16 + (pz // 2) * 8 + px * 2 + pc
                        pairs.append((me, to))
    return lax.ppermute(a, AXES, pairs)


def over_x(a, first):
    return swap(a, lambda x, y, z, c: (x ^ (XA if (c == 0) == first else XB), y, z, c))


def over_z(a):
    return swap(a, lambda x, y, z, c: (x, y, z ^ 3, c))


def over_core(a):
    return swap(a, lambda x, y, z, c: (x, y, z, c ^ 1))


def over_island(a, mask, other=None):
    masks = (mask, mask if other is None else other)
    return swap(a, lambda x, y, z, c: (x, y ^ (masks[c] & 3), z ^ (masks[c] >> 2), c))


def slope(product, scale, factor):
    half = product * (0.5 * scale)
    bent = jnp.tanh(half)
    return (bent * (0.5 * factor) + 0.5 * factor) * (1.0 + half * (1.0 - bent))


def turn_cotangent(where, cot, ids):
    steps, tokens, hidden_units = cot.shape
    units = hidden_units // 8
    n = 8

    def kernel(where_ref, cot_ref, ids_ref, *refs):
        outs, held, turned, digits, in_sems, out_sems = refs[:n], *refs[n:]
        loads = []
        for s in range(steps):
            load = pltpu.make_async_copy(cot_ref.at[s], held.at[s], in_sems.at[s])
            load.start()
            loads.append(load)
        row = lax.broadcasted_iota(jnp.int32, (IDS, tokens), 0)
        rows = jnp.zeros((IDS, tokens), jnp.int32)
        for s in range(steps):
            one = ids_ref[s : s + 1, :]
            rows = jnp.where(row == 2 * s, one >> 8, jnp.where(row == 2 * s + 1, one & 255, rows))
        digits[...] = rows.astype(jnp.float32).astype(jnp.bfloat16)
        stores = []

        def store(source, target):
            copy = pltpu.make_async_copy(source, target, out_sems.at[len(stores)])
            copy.start()
            stores.append(copy)

        for m in range(n):
            store(digits, outs[m].at[pl.ds(steps * units, IDS), :])
        for s in range(steps):
            loads[s].wait()
            for col in range(0, hidden_units, 128):
                turned[s, col : col + 128, :] = held[s, :, col : col + 128].T
            for m in range(n):
                at = row_of(where_ref, jnp.where((where_ref[1] & 1) == 0, MASKS[0][m], MASKS[1][m]), units)
                store(turned.at[s, pl.ds(at, units), :], outs[m].at[pl.ds(s * units, units), :])
        for copy in stores:
            copy.wait()

    return pl.pallas_call(
        kernel,
        in_specs=[
            pl.BlockSpec(memory_space=pltpu.SMEM),
            pl.BlockSpec(memory_space=pltpu.HBM),
            pl.BlockSpec(memory_space=pltpu.VMEM),
        ],
        out_specs=[pl.BlockSpec(memory_space=pltpu.HBM)] * n,
        out_shape=[jax.ShapeDtypeStruct((steps * units + IDS, tokens), cot.dtype)] * n,
        scratch_shapes=[
            pltpu.VMEM((steps, tokens, hidden_units), cot.dtype),
            pltpu.VMEM((steps, hidden_units, tokens), cot.dtype),
            pltpu.VMEM((IDS, tokens), cot.dtype),
            pltpu.SemaphoreType.DMA((steps,)),
            pltpu.SemaphoreType.DMA((n * (steps + 1),)),
        ],
        compiler_params=pltpu.CompilerParams(vmem_limit_bytes=VMEM_ALL),
        cost_estimate=small(),
        name="turn_cotangent",
    )(where, cot, ids)


def own_rows(where, weights, momentum, after):
    width, hidden_units = weights.shape
    units = hidden_units // 8

    def kernel(where_ref, w_ref, m_ref, _, w_out, m_out, held, turned, sems):
        stores = []
        low, shift = window_of(where_ref, 0, units)
        cols, rows = pl.ds(low, 256), pl.ds(shift, units)
        loads = []
        for k, ref in enumerate((w_ref, m_ref)):
            load = pltpu.make_async_copy(ref.at[:, cols], held.at[k], sems.at[k])
            load.start()
            loads.append(load)
        for k, out in enumerate((w_out, m_out)):
            loads[k].wait()
            for at in range(0, width, 512):
                turned[k, :, at : at + 512] = held[k, at : at + 512, :].T
            store = pltpu.make_async_copy(turned.at[k, rows, :], out, sems.at[2 + k])
            store.start()
            stores.append(store)
        for store in stores:
            store.wait()

    return pl.pallas_call(
        kernel,
        in_specs=[pl.BlockSpec(memory_space=pltpu.SMEM)] + [pl.BlockSpec(memory_space=pltpu.HBM)] * 3,
        out_specs=[pl.BlockSpec(memory_space=pltpu.HBM)] * 2,
        out_shape=[jax.ShapeDtypeStruct((units, width), weights.dtype)] * 2,
        scratch_shapes=[
            pltpu.VMEM((2, width, 256), weights.dtype),
            pltpu.VMEM((2, 256, width), weights.dtype),
            pltpu.SemaphoreType.DMA((4,)),
        ],
        compiler_params=pltpu.CompilerParams(vmem_limit_bytes=VMEM_ALL),
        cost_estimate=small(),
        name="own_rows",
    )(where, weights, momentum, *after)


def add_by_row(arrived, rows, steps):
    n = len(arrived)
    tokens = arrived[0].shape[1]
    units = (arrived[0].shape[0] - IDS) // steps
    highs = rows // 256

    def kernel(*refs):
        sources, targets, messages, sums, in_sems, out_sems = refs[:n], refs[n : n + steps], *refs[n + steps :]
        loads = [pltpu.make_async_copy(sources[m], messages.at[m], in_sems.at[m]) for m in range(n)]
        for load in loads:
            load.start()
        stores = []
        row = lax.broadcasted_iota(jnp.int32, (256, tokens), 0).astype(jnp.float32)
        for m in range(n):
            loads[m].wait()
            digits = messages[m, steps * units : steps * units + IDS, :].astype(jnp.float32)
            for step in range(steps):
                high, low = digits[2 * step : 2 * step + 1], digits[2 * step + 1 : 2 * step + 2]
                hot = jnp.where(low == row, 1.0, 0.0).astype(jnp.bfloat16)
                cot = messages[m, step * units : (step + 1) * units, :]
                parted = [cot * jnp.where(high == float(k), 1.0, 0.0).astype(jnp.bfloat16) for k in range(highs)]
                total = lax.dot_general(
                    jnp.concatenate(parted), hot, (((1,), (1,)), ((), ())), preferred_element_type=jnp.float32
                ).astype(jnp.bfloat16)
                for k in range(highs):
                    sums[m, step, :, k * 256 : (k + 1) * 256] = total[k * units : (k + 1) * units]
                store = pltpu.make_async_copy(
                    sums.at[m, step], targets[step].at[pl.ds(m * units, units), :], out_sems.at[m * steps + step]
                )
                store.start()
                stores.append(store)
        for store in stores:
            store.wait()

    return pl.pallas_call(
        kernel,
        in_specs=[pl.BlockSpec(memory_space=pltpu.HBM)] * n,
        out_specs=[pl.BlockSpec(memory_space=pltpu.HBM)] * steps,
        out_shape=[jax.ShapeDtypeStruct((n * units, rows), jnp.bfloat16)] * steps,
        scratch_shapes=[
            pltpu.VMEM((n, *arrived[0].shape), jnp.bfloat16),
            pltpu.VMEM((n, steps, units, rows), jnp.bfloat16),
            pltpu.SemaphoreType.DMA((n,)),
            pltpu.SemaphoreType.DMA((n * steps,)),
        ],
        compiler_params=pltpu.CompilerParams(vmem_limit_bytes=VMEM_ALL),
        cost_estimate=pl.CostEstimate(flops=n * 10**9, bytes_accessed=n * MB, transcendentals=0),
        name="add_by_row",
    )(*arrived)


def together(*arrays):
    n = len(arrays)
    return pl.pallas_call(
        lambda *refs: None,
        in_specs=[pl.BlockSpec(memory_space=pltpu.HBM)] * n,
        out_specs=[pl.BlockSpec(memory_space=pltpu.HBM)] * n,
        out_shape=[jax.ShapeDtypeStruct(a.shape, a.dtype) for a in arrays],
        input_output_aliases={k: k for k in range(n)},
        compiler_params=pltpu.CompilerParams(vmem_limit_bytes=VMEM_ALL),
        cost_estimate=small(),
        name="together",
    )(*arrays)


def pack(arrays):
    n, (count, width) = len(arrays), arrays[0].shape

    def kernel(*refs):
        sources, out, held, in_sems, out_sems = refs[:n], *refs[n:]
        loads, stores = [], []
        for k in range(n):
            loads.append(pltpu.make_async_copy(sources[k], held.at[k], in_sems.at[k]))
            stores.append(pltpu.make_async_copy(held.at[k], out.at[pl.ds(k * count, count), :], out_sems.at[k]))
            loads[k].start()
        for load, store in zip(loads, stores):
            load.wait()
            store.start()
        for store in stores:
            store.wait()

    return pl.pallas_call(
        kernel,
        in_specs=[pl.BlockSpec(memory_space=pltpu.HBM)] * n,
        out_specs=pl.BlockSpec(memory_space=pltpu.HBM),
        out_shape=jax.ShapeDtypeStruct((n * count, width), arrays[0].dtype),
        scratch_shapes=[
            pltpu.VMEM((n, count, width), arrays[0].dtype),
            pltpu.SemaphoreType.DMA((n,)),
            pltpu.SemaphoreType.DMA((n,)),
        ],
        compiler_params=pltpu.CompilerParams(vmem_limit_bytes=VMEM_ALL),
        cost_estimate=small(),
        name="pack",
    )(*arrays)


def places(rows, x, core, zhi):
    found = []
    for q in range(2):
        cc = core ^ q
        d1 = XA + (XB - XA) * cc
        order = ((x, 0), (x ^ d1, 0), (x ^ d1 ^ 2, 0), (x, 1), (x ^ 2, 0), (x ^ d1, 1), (x ^ d1 ^ 2, 1), (x ^ 2, 1))
        for k, (xx, zz) in enumerate(order):
            piece, first = (k, 0) if q == 0 else ((8, 0), (9, 0), (8, 1), (8, 2), (10, 0), (11, 0), (12, 0), (13, 0))[k]
            found.append((piece, first * rows, 256 * ((zhi ^ zz) * 8 + xx * 2 + cc)))
    return found


def main_steps(pieces, position, w, momentum, cots, tokens):
    rows = cots[0][0].shape[1]
    units, width = w.shape
    many = 8 * units
    scale = 1.0 / math.sqrt(width)
    first_0 = beta_one * (1.0 - beta_one) / (1.0 - beta_one**2)
    first_1 = (1.0 - beta_one) / (1.0 - beta_one**2)
    root_0 = math.sqrt(beta_two * (1.0 - beta_two) / (1.0 - beta_two**2))
    root_1 = math.sqrt((1.0 - beta_two) / (1.0 - beta_two**2))
    weight_0, weight_1 = first_0 / root_0, first_1 / root_1
    eps = adam_eps / scale
    narrow = jnp.bfloat16
    half = (slice(0, many // 2), slice(many // 2, many))
    keep = 1.0 - inner_rate * decay_rate
    block, wide = 1024, 2048
    n, sets = len(pieces), len(cots)

    def kernel(where_ref, *refs):
        piece_refs, (w_hbm, mom_hbm), refs = refs[:n], refs[n : n + 2], refs[n + 2 :]
        cot_hbm, out_ref, refs = refs[: 2 * sets], refs[2 * sets], refs[2 * sets + 1 :]
        table, work, grads, up, cot, ratio, hidden, w_ref, mom_ref, sems, more = refs
        flat = places(rows, (where_ref[1] >> 1) & 3, where_ref[1] & 1, where_ref[1] >> 3)
        columns = [pl.multiple_of(col, 256) for _, _, col in flat]

        def start(source, target, sem):
            copy = pltpu.make_async_copy(source, target, sem)
            copy.start()
            return copy

        def load_cots(step):
            loads, at = [], 0
            for k in range(sets):
                size = cots[k][step].shape[0]
                loads.append(start(cot_hbm[2 * k + step], cot.at[pl.ds(at, size), :], more.at[2 + k]))
                at += size
            return loads

        load_w = start(w_hbm, w_ref, more.at[0])
        copies = []
        for k, (piece, first, _) in enumerate(flat):
            copies.append(
                start(piece_refs[piece].at[pl.ds(first, rows), :], table.at[:, pl.ds(columns[k], 256)], sems.at[k])
            )
            if k == 8:
                load_c = load_cots(0)
                load_m = start(mom_hbm, mom_ref, more.at[1])
        load_w.wait()
        for k in range(16):
            copies[k].wait()
            cols = pl.ds(columns[k], 256)
            part = lax.dot_general(
                w_ref[:, cols], table[:, cols], (((1,), (1,)), ((), ())), preferred_element_type=jnp.float32
            )
            if k == 0:
                hidden[...] = part
            else:
                hidden[...] += part
        for load in load_c:
            load.wait()
        for at in range(0, rows, block):
            cols = slice(at, at + block)
            factor = slope(hidden[:, cols], scale, root_0 / tokens)
            for m in range(8):
                span = slice(m * units, (m + 1) * units)
                up[span, cols] = (cot[span, cols].astype(jnp.float32) * factor).astype(jnp.bfloat16)
        load_c = load_cots(1)

        @pl.loop(0, width // wide)
        def _(i):
            cols = pl.ds(pl.multiple_of(i * wide, wide), wide)
            halves = [jnp.dot(up[at, :], table[:, cols], preferred_element_type=jnp.float32) for at in half]
            kept = w_ref[:, cols].astype(jnp.float32) * keep
            total = jnp.zeros(kept.shape, jnp.float32)
            for m in range(8):
                span = slice(m * units, (m + 1) * units)
                g = halves[m // 4][m % 4 * units : (m % 4 + 1) * units]
                r = g * pl.reciprocal(jnp.abs(g) + eps * root_0, approx=True)
                total = total + r
                work[span, cols] = (kept - inner_rate * r).astype(jnp.bfloat16)
                grads[span, cols] = g.astype(jnp.bfloat16)
            ratio[:, cols] = total

        for load in load_c:
            load.wait()

        @pl.loop(0, rows // block)
        def _(t):
            at = pl.ds(pl.multiple_of(t * block, block), block)
            products = [
                lax.dot_general(
                    work[rows_of, :], table[at, :], (((1,), (1,)), ((), ())), preferred_element_type=jnp.float32
                )
                for rows_of in half
            ]
            for rows_of, product in zip(half, products):
                up[rows_of, at] = (cot[rows_of, at].astype(jnp.float32) * slope(product, scale, root_1 / tokens)).astype(
                    jnp.bfloat16
                )

        load_m.wait()

        @pl.loop(0, width // wide)
        def _(i):
            cols = pl.ds(pl.multiple_of(i * wide, wide), wide)
            halves = [jnp.dot(up[at, :], table[:, cols], preferred_element_type=jnp.float32) for at in half]
            start_w = w_ref[:, cols].astype(jnp.float32)
            total = jnp.zeros(start_w.shape, jnp.float32)
            for m in range(8):
                span = slice(m * units, (m + 1) * units)
                b = halves[m // 4][m % 4 * units : (m % 4 + 1) * units].astype(narrow)
                a = grads[span, cols]
                v = a * a + b * b + narrow(1e-30)
                r = (a + narrow(weight_1 / weight_0) * b) * pl.reciprocal(
                    v * lax.rsqrt(v) + narrow(eps), approx=True
                )
                total = total + r.astype(jnp.float32)
            mean = (1.0 - keep * keep) * start_w + (inner_rate / 8.0) * (keep * ratio[:, cols] + weight_0 * total)
            moment = outer_moment * mom_ref[:, cols].astype(jnp.float32) + mean
            out_ref[:, cols] = (start_w - outer_rate * (mean + outer_moment * moment)).astype(jnp.bfloat16)

    return pl.pallas_call(
        kernel,
        in_specs=[pl.BlockSpec(memory_space=pltpu.SMEM)] + [pl.BlockSpec(memory_space=pltpu.HBM)] * (n + 2 + 2 * sets),
        out_specs=pl.BlockSpec(memory_space=pltpu.VMEM),
        out_shape=jax.ShapeDtypeStruct((units, width), jnp.bfloat16),
        scratch_shapes=[
            pltpu.VMEM((rows, width), jnp.bfloat16),
            pltpu.VMEM((many, width), jnp.bfloat16),
            pltpu.VMEM((many, width), jnp.bfloat16),
            pltpu.VMEM((many, rows), jnp.bfloat16),
            pltpu.VMEM((many, rows), jnp.bfloat16),
            pltpu.VMEM((units, width), jnp.float32),
            pltpu.VMEM((units, rows), jnp.float32),
            pltpu.VMEM((units, width), jnp.bfloat16),
            pltpu.VMEM((units, width), jnp.bfloat16),
            pltpu.SemaphoreType.DMA((16,)),
            pltpu.SemaphoreType.DMA((2 + sets,)),
        ],
        compiler_params=pltpu.CompilerParams(vmem_limit_bytes=VMEM_ALL),
        cost_estimate=pl.CostEstimate(flops=52 * units * rows * width, bytes_accessed=rows * width * 2, transcendentals=0),
        name="main_steps",
    )(position, *pieces, w, momentum, *(c for pair in cots for c in pair))


def spread(new):
    e1, e2, e3 = LINKS
    near = [over_island(new, e) for e in LINKS]
    far = [over_island(near[1], e1), over_island(near[2], e2), over_island(near[0], e3)]
    found = [(new, 0), (near[0], e1), (near[1], e2), (near[2], e3)]
    found += [(far[0], e1 ^ e2), (far[1], e2 ^ e3), (far[2], e1 ^ e3)]
    last = []
    for (low, size), source, e in zip(PARTS, (far[1], far[2], far[0]), LINKS):
        last.append((over_island(source[:, low : low + size], e), low))
    return found, last


def assemble(found, where, units, width):
    n = len(found)

    def kernel(where_ref, *refs):
        arrays, out, held, turned, sems, out_sems = refs[:n], *refs[n:]
        waits = []
        for p, (low, length) in enumerate(TURNS):
            copies = []
            for k, (_, mask) in enumerate(found):
                row = row_of(where_ref, mask, units)
                part = pl.ds(low, length)
                copy = pltpu.make_async_copy(
                    arrays[k].at[:, part], held.at[pl.ds(row, units), part], sems.at[p, k]
                )
                copy.start()
                copies.append(copy)
            waits.append(copies)
        row = row_of(where_ref, LAST, units)
        held[pl.ds(row, units), :] = jnp.zeros((units, width), held.dtype)
        outs = []
        for p, (low, length) in enumerate(TURNS):
            for copy in waits[p]:
                copy.wait()
            for col in range(low, low + length, 128):
                turned[col : col + 128, :] = held[:, col : col + 128].T
            copy = pltpu.make_async_copy(
                turned.at[pl.ds(low, length), :], out.at[pl.ds(low, length), :], out_sems.at[p]
            )
            copy.start()
            outs.append(copy)
        for copy in outs:
            copy.wait()

    return pl.pallas_call(
        kernel,
        in_specs=[pl.BlockSpec(memory_space=pltpu.SMEM)] + [pl.BlockSpec(memory_space=pl.ANY)] * n,
        out_specs=pl.BlockSpec(memory_space=pltpu.HBM),
        out_shape=jax.ShapeDtypeStruct((width, 8 * units), jnp.bfloat16),
        scratch_shapes=[
            pltpu.VMEM((8 * units, width), jnp.bfloat16),
            pltpu.VMEM((width, 8 * units), jnp.bfloat16),
            pltpu.SemaphoreType.DMA((len(TURNS), n)),
            pltpu.SemaphoreType.DMA((len(TURNS),)),
        ],
        compiler_params=pltpu.CompilerParams(vmem_limit_bytes=24 * MB),
        cost_estimate=pl.CostEstimate(flops=0, bytes_accessed=32 * units * width, transcendentals=0),
        name="assemble",
    )(where, *(array for array, _ in found))


def complete(whole, last, where, units, width):
    n = len(last)
    window = 256

    def kernel(where_ref, whole_ref, *refs):
        arrays, out, kept, held, merged, in_sems, sems, out_sems = refs[:n], *refs[n:]
        low, shift = window_of(where_ref, LAST, units)
        cols = pl.ds(low, window)
        loads, arrivals = [], []
        for k, (array, low) in enumerate(last):
            part = pl.ds(low, array.shape[1])
            arrival = pltpu.make_async_copy(arrays[k], held.at[pl.ds(shift, units), part], sems.at[k])
            load = pltpu.make_async_copy(whole_ref.at[part, cols], kept.at[part, :], in_sems.at[k])
            arrival.start()
            load.start()
            loads.append(load)
            arrivals.append(arrival)
        lane = lax.broadcasted_iota(jnp.int32, (128, window), 1)
        ours = (lane >= shift) & (lane < shift + units)
        stores = []
        for k, (array, low) in enumerate(last):
            loads[k].wait()
            arrivals[k].wait()
            for col in range(low, low + array.shape[1], 128):
                here = slice(col, col + 128)
                merged[here, :] = jnp.where(ours, held[:, here].T.astype(jnp.float32), kept[here, :].astype(jnp.float32)).astype(
                    merged.dtype
                )
            part = pl.ds(low, array.shape[1])
            store = pltpu.make_async_copy(merged.at[part, :], out.at[part, cols], out_sems.at[k])
            store.start()
            stores.append(store)
        for store in stores:
            store.wait()

    return pl.pallas_call(
        kernel,
        in_specs=[pl.BlockSpec(memory_space=pltpu.SMEM), pl.BlockSpec(memory_space=pltpu.HBM)]
        + [pl.BlockSpec(memory_space=pl.ANY)] * n,
        out_specs=pl.BlockSpec(memory_space=pltpu.HBM),
        out_shape=jax.ShapeDtypeStruct(whole.shape, whole.dtype),
        input_output_aliases={1: 0},
        scratch_shapes=[
            pltpu.VMEM((width, window), whole.dtype),
            pltpu.VMEM((window, width), whole.dtype),
            pltpu.VMEM((width, window), whole.dtype),
            pltpu.SemaphoreType.DMA((n,)),
            pltpu.SemaphoreType.DMA((n,)),
            pltpu.SemaphoreType.DMA((n,)),
        ],
        compiler_params=pltpu.CompilerParams(vmem_limit_bytes=16 * MB),
        cost_estimate=small(),
        name="complete",
    )(where, whole, *(array for array, _ in last))


def body(weights, momentum, table, token_ids, cotangent):
    island, fsdp = lax.axis_index("island"), lax.axis_index("fsdp")
    width, hidden_units = weights.shape
    steps, tokens = token_ids.shape[1:]
    rows = table.shape[0]
    units = hidden_units // 8
    where = jnp.stack([island, fsdp]).astype(jnp.int32)

    def exchange(k):
        return over_island(m[k], MASKS[0][k], MASKS[1][k])

    z, x1, x2 = over_z(table), over_x(table, True), over_x(table, False)
    m = list(turn_cotangent(where, cotangent[0], token_ids[0]))
    w, mom = own_rows(where, weights, momentum, m[:1])
    k1, k2 = exchange(1), exchange(2)
    z, x1, x2, k1, k2, w, mom, *m[3:] = together(z, x1, x2, k1, k2, w, mom, *m[3:])

    x1z, x3, x2z, k3 = over_z(x1), over_x(x1, False), over_x(z, False), exchange(3)
    x1_o = over_core(x1)
    c0, c1 = add_by_row([m[0], k1, k2], rows, steps)
    k3, x1_o, m[4], m[5] = together(k3, x1_o, m[4], m[5])
    k4, k5 = exchange(4), exchange(5)
    early = pack([table, x2, z])
    x1z, x3, x2z, k4, k5, early, c0, c1, *m[6:] = together(x1z, x3, x2z, k4, k5, early, c0, c1, *m[6:])
    cots = [(c0, c1)]

    x3z, k6, k7, early_o = over_x(x1z, False), exchange(6), exchange(7), over_core(early)
    x3_o = over_core(x3)
    c0, c1 = add_by_row([k3, k4, k5], rows, steps)
    x3z, k6, k7, early_o, x3_o, c0, c1 = together(x3z, k6, k7, early_o, x3_o, c0, c1)
    cots.append((c0, c1))

    others = [early_o, x1_o, x3_o, over_core(x1z), over_core(x2z), over_core(x3z)]
    cots.append(add_by_row([k6, k7], rows, steps))
    pieces = [table, x1, x2, z, x3, x1z, x2z, x3z, *others]
    new = main_steps(pieces, where, w, mom, cots, tokens)
    found, last = spread(new)
    return complete(assemble(found, where, units, width), last, where, units, width)


def solution(mesh):
    placed = (
        P(None, "fsdp"),
        P(None, "fsdp"),
        P(None, "fsdp"),
        P("island", None, None),
        P("island", None, None, "fsdp"),
    )
    return jax.shard_map(body, mesh=mesh, in_specs=placed, out_specs=P(None, "fsdp"), check_vma=False)
```

```python
import math

import jax
import jax.numpy as jnp
from jax import lax
from jax.experimental import pallas as pl
from jax.experimental.pallas import tpu as pltpu
from jax.sharding import PartitionSpec as P

beta_one = 0.9
beta_two = 0.95
adam_eps = 0.0001
inner_rate = 0.1
decay_rate = 0.1
outer_rate = 0.7
outer_moment = 0.9

MB = 1 << 20
AXES = ("island", "fsdp")
XA, XB = 1, 3
MASKS = ((0, 5, 1, 6, 4, 2, 7, 3), (0, 7, 3, 6, 4, 2, 5, 1))
PARTS = ((0, 1408), (1408, 1408), (2816, 1280))
TURNS = ((0, 768), (768, 640), (1408, 768), (2176, 640), (2816, 640), (3456, 640))
LAST = 6
LINKS = (1, 3, 4)
VMEM_ALL = 64 * MB - 256 * 1024
IDS = 16


def row_of(where_ref, mask, units):
    return pl.multiple_of((where_ref[0] ^ mask) * units, 16)


def window_of(where_ref, mask, units):
    first = (where_ref[0] ^ mask) * units
    low = jnp.minimum(first >> 7, 8 * units // 128 - 2) * 128
    return pl.multiple_of(low, 128), pl.multiple_of(first - low, 16)


def small():
    return pl.CostEstimate(flops=0, bytes_accessed=1024, transcendentals=0)


def swap(a, partner):
    pairs = []
    for zlo in range(2):
        for y in range(4):
            for zhi in range(2):
                for x in range(4):
                    for c in range(2):
                        px, py, pz, pc = partner(x, y, zhi * 2 + zlo, c)
                        me = (zlo * 4 + y) * 16 + zhi * 8 + x * 2 + c
                        to = ((pz % 2) * 4 + py) * 16 + (pz // 2) * 8 + px * 2 + pc
                        pairs.append((me, to))
    return lax.ppermute(a, AXES, pairs)


def over_x(a, first):
    return swap(a, lambda x, y, z, c: (x ^ (XA if (c == 0) == first else XB), y, z, c))


def over_z(a):
    return swap(a, lambda x, y, z, c: (x, y, z ^ 3, c))


def over_core(a):
    return swap(a, lambda x, y, z, c: (x, y, z, c ^ 1))


def over_island(a, mask, other=None):
    masks = (mask, mask if other is None else other)
    return swap(a, lambda x, y, z, c: (x, y ^ (masks[c] & 3), z ^ (masks[c] >> 2), c))


def slope(product, scale, factor):
    half = product * (0.5 * scale)
    bent = jnp.tanh(half)
    return (bent * (0.5 * factor) + 0.5 * factor) * (1.0 + half * (1.0 - bent))


def turn_cotangent(where, cot, ids):
    steps, tokens, hidden_units = cot.shape
    units = hidden_units // 8
    n = 8

    def kernel(where_ref, cot_ref, ids_ref, *refs):
        outs, held, turned, digits, in_sems, out_sems = refs[:n], *refs[n:]
        loads = []
        for s in range(steps):
            load = pltpu.make_async_copy(cot_ref.at[s], held.at[s], in_sems.at[s])
            load.start()
            loads.append(load)
        row = lax.broadcasted_iota(jnp.int32, (IDS, tokens), 0)
        rows = jnp.zeros((IDS, tokens), jnp.int32)
        for s in range(steps):
            one = ids_ref[s : s + 1, :]
            rows = jnp.where(row == 2 * s, one >> 8, jnp.where(row == 2 * s + 1, one & 255, rows))
        digits[...] = rows.astype(jnp.float32).astype(jnp.bfloat16)
        stores = []

        def store(source, target):
            copy = pltpu.make_async_copy(source, target, out_sems.at[len(stores)])
            copy.start()
            stores.append(copy)

        for m in range(n):
            store(digits, outs[m].at[pl.ds(steps * units, IDS), :])
        for s in range(steps):
            loads[s].wait()
            for col in range(0, hidden_units, 128):
                turned[s, col : col + 128, :] = held[s, :, col : col + 128].T
            for m in range(n):
                at = row_of(where_ref, jnp.where((where_ref[1] & 1) == 0, MASKS[0][m], MASKS[1][m]), units)
                store(turned.at[s, pl.ds(at, units), :], outs[m].at[pl.ds(s * units, units), :])
        for copy in stores:
            copy.wait()

    return pl.pallas_call(
        kernel,
        in_specs=[
            pl.BlockSpec(memory_space=pltpu.SMEM),
            pl.BlockSpec(memory_space=pltpu.HBM),
            pl.BlockSpec(memory_space=pltpu.VMEM),
        ],
        out_specs=[pl.BlockSpec(memory_space=pltpu.HBM)] * n,
        out_shape=[jax.ShapeDtypeStruct((steps * units + IDS, tokens), cot.dtype)] * n,
        scratch_shapes=[
            pltpu.VMEM((steps, tokens, hidden_units), cot.dtype),
            pltpu.VMEM((steps, hidden_units, tokens), cot.dtype),
            pltpu.VMEM((IDS, tokens), cot.dtype),
            pltpu.SemaphoreType.DMA((steps,)),
            pltpu.SemaphoreType.DMA((n * (steps + 1),)),
        ],
        compiler_params=pltpu.CompilerParams(vmem_limit_bytes=VMEM_ALL),
        cost_estimate=small(),
        name="turn_cotangent",
    )(where, cot, ids)


def own_rows(where, weights, momentum, after):
    width, hidden_units = weights.shape
    units = hidden_units // 8

    def kernel(where_ref, w_ref, m_ref, _, w_out, m_out, held, turned, sems):
        stores = []
        low, shift = window_of(where_ref, 0, units)
        cols, rows = pl.ds(low, 256), pl.ds(shift, units)
        loads = []
        for k, ref in enumerate((w_ref, m_ref)):
            load = pltpu.make_async_copy(ref.at[:, cols], held.at[k], sems.at[k])
            load.start()
            loads.append(load)
        for k, out in enumerate((w_out, m_out)):
            loads[k].wait()
            for at in range(0, width, 512):
                turned[k, :, at : at + 512] = held[k, at : at + 512, :].T
            store = pltpu.make_async_copy(turned.at[k, rows, :], out, sems.at[2 + k])
            store.start()
            stores.append(store)
        for store in stores:
            store.wait()

    return pl.pallas_call(
        kernel,
        in_specs=[pl.BlockSpec(memory_space=pltpu.SMEM)] + [pl.BlockSpec(memory_space=pltpu.HBM)] * 3,
        out_specs=[pl.BlockSpec(memory_space=pltpu.HBM)] * 2,
        out_shape=[jax.ShapeDtypeStruct((units, width), weights.dtype)] * 2,
        scratch_shapes=[
            pltpu.VMEM((2, width, 256), weights.dtype),
            pltpu.VMEM((2, 256, width), weights.dtype),
            pltpu.SemaphoreType.DMA((4,)),
        ],
        compiler_params=pltpu.CompilerParams(vmem_limit_bytes=VMEM_ALL),
        cost_estimate=small(),
        name="own_rows",
    )(where, weights, momentum, *after)


def add_by_row(arrived, rows, steps):
    n = len(arrived)
    tokens = arrived[0].shape[1]
    units = (arrived[0].shape[0] - IDS) // steps
    highs = rows // 256

    def kernel(*refs):
        sources, targets, messages, sums, in_sems, out_sems = refs[:n], refs[n : n + steps], *refs[n + steps :]
        loads = [pltpu.make_async_copy(sources[m], messages.at[m], in_sems.at[m]) for m in range(n)]
        for load in loads:
            load.start()
        stores = []
        row = lax.broadcasted_iota(jnp.int32, (256, tokens), 0).astype(jnp.float32)
        for m in range(n):
            loads[m].wait()
            digits = messages[m, steps * units : steps * units + IDS, :].astype(jnp.float32)
            for step in range(steps):
                high, low = digits[2 * step : 2 * step + 1], digits[2 * step + 1 : 2 * step + 2]
                hot = jnp.where(low == row, 1.0, 0.0).astype(jnp.bfloat16)
                cot = messages[m, step * units : (step + 1) * units, :]
                parted = [cot * jnp.where(high == float(k), 1.0, 0.0).astype(jnp.bfloat16) for k in range(highs)]
                total = lax.dot_general(
                    jnp.concatenate(parted), hot, (((1,), (1,)), ((), ())), preferred_element_type=jnp.float32
                ).astype(jnp.bfloat16)
                for k in range(highs):
                    sums[m, step, :, k * 256 : (k + 1) * 256] = total[k * units : (k + 1) * units]
                store = pltpu.make_async_copy(
                    sums.at[m, step], targets[step].at[pl.ds(m * units, units), :], out_sems.at[m * steps + step]
                )
                store.start()
                stores.append(store)
        for store in stores:
            store.wait()

    return pl.pallas_call(
        kernel,
        in_specs=[pl.BlockSpec(memory_space=pltpu.HBM)] * n,
        out_specs=[pl.BlockSpec(memory_space=pltpu.HBM)] * steps,
        out_shape=[jax.ShapeDtypeStruct((n * units, rows), jnp.bfloat16)] * steps,
        scratch_shapes=[
            pltpu.VMEM((n, *arrived[0].shape), jnp.bfloat16),
            pltpu.VMEM((n, steps, units, rows), jnp.bfloat16),
            pltpu.SemaphoreType.DMA((n,)),
            pltpu.SemaphoreType.DMA((n * steps,)),
        ],
        compiler_params=pltpu.CompilerParams(vmem_limit_bytes=VMEM_ALL),
        cost_estimate=pl.CostEstimate(flops=n * 10**9, bytes_accessed=n * MB, transcendentals=0),
        name="add_by_row",
    )(*arrived)


def together(*arrays):
    n = len(arrays)
    return pl.pallas_call(
        lambda *refs: None,
        in_specs=[pl.BlockSpec(memory_space=pltpu.HBM)] * n,
        out_specs=[pl.BlockSpec(memory_space=pltpu.HBM)] * n,
        out_shape=[jax.ShapeDtypeStruct(a.shape, a.dtype) for a in arrays],
        input_output_aliases={k: k for k in range(n)},
        compiler_params=pltpu.CompilerParams(vmem_limit_bytes=VMEM_ALL),
        cost_estimate=small(),
        name="together",
    )(*arrays)


def pack(arrays):
    n, (count, width) = len(arrays), arrays[0].shape

    def kernel(*refs):
        sources, out, held, in_sems, out_sems = refs[:n], *refs[n:]
        loads, stores = [], []
        for k in range(n):
            loads.append(pltpu.make_async_copy(sources[k], held.at[k], in_sems.at[k]))
            stores.append(pltpu.make_async_copy(held.at[k], out.at[pl.ds(k * count, count), :], out_sems.at[k]))
            loads[k].start()
        for load, store in zip(loads, stores):
            load.wait()
            store.start()
        for store in stores:
            store.wait()

    return pl.pallas_call(
        kernel,
        in_specs=[pl.BlockSpec(memory_space=pltpu.HBM)] * n,
        out_specs=pl.BlockSpec(memory_space=pltpu.HBM),
        out_shape=jax.ShapeDtypeStruct((n * count, width), arrays[0].dtype),
        scratch_shapes=[
            pltpu.VMEM((n, count, width), arrays[0].dtype),
            pltpu.SemaphoreType.DMA((n,)),
            pltpu.SemaphoreType.DMA((n,)),
        ],
        compiler_params=pltpu.CompilerParams(vmem_limit_bytes=VMEM_ALL),
        cost_estimate=small(),
        name="pack",
    )(*arrays)


def places(rows, x, core, zhi):
    found = []
    for q in range(2):
        cc = core ^ q
        d1 = XA + (XB - XA) * cc
        order = ((x, 0), (x ^ d1, 0), (x ^ d1 ^ 2, 0), (x, 1), (x ^ 2, 0), (x ^ d1, 1), (x ^ d1 ^ 2, 1), (x ^ 2, 1))
        for k, (xx, zz) in enumerate(order):
            piece, first = (k, 0) if q == 0 else ((8, 0), (9, 0), (8, 1), (8, 2), (10, 0), (11, 0), (12, 0), (13, 0))[k]
            found.append((piece, first * rows, 256 * ((zhi ^ zz) * 8 + xx * 2 + cc)))
    return found


def main_steps(pieces, position, w, momentum, cots, tokens):
    rows = cots[0][0].shape[1]
    units, width = w.shape
    many = 8 * units
    scale = 1.0 / math.sqrt(width)
    first_0 = beta_one * (1.0 - beta_one) / (1.0 - beta_one**2)
    first_1 = (1.0 - beta_one) / (1.0 - beta_one**2)
    root_0 = math.sqrt(beta_two * (1.0 - beta_two) / (1.0 - beta_two**2))
    root_1 = math.sqrt((1.0 - beta_two) / (1.0 - beta_two**2))
    weight_0, weight_1 = first_0 / root_0, first_1 / root_1
    eps = adam_eps / scale
    narrow = jnp.bfloat16
    half = (slice(0, many // 2), slice(many // 2, many))
    keep = 1.0 - inner_rate * decay_rate
    block, wide = 1024, 2048
    n, sets = len(pieces), len(cots)

    def kernel(where_ref, *refs):
        piece_refs, (w_hbm, mom_hbm), refs = refs[:n], refs[n : n + 2], refs[n + 2 :]
        cot_hbm, out_ref, refs = refs[: 2 * sets], refs[2 * sets], refs[2 * sets + 1 :]
        table, work, grads, up, cot, ratio, hidden, w_ref, mom_ref, sems, more = refs
        flat = places(rows, (where_ref[1] >> 1) & 3, where_ref[1] & 1, where_ref[1] >> 3)
        columns = [pl.multiple_of(col, 256) for _, _, col in flat]

        def start(source, target, sem):
            copy = pltpu.make_async_copy(source, target, sem)
            copy.start()
            return copy

        def load_cots(step):
            loads, at = [], 0
            for k in range(sets):
                size = cots[k][step].shape[0]
                loads.append(start(cot_hbm[2 * k + step], cot.at[pl.ds(at, size), :], more.at[2 + k]))
                at += size
            return loads

        load_w = start(w_hbm, w_ref, more.at[0])
        copies = []
        for k, (piece, first, _) in enumerate(flat):
            copies.append(
                start(piece_refs[piece].at[pl.ds(first, rows), :], table.at[:, pl.ds(columns[k], 256)], sems.at[k])
            )
            if k == 8:
                load_c = load_cots(0)
                load_m = start(mom_hbm, mom_ref, more.at[1])
        load_w.wait()
        for k in range(16):
            copies[k].wait()
            cols = pl.ds(columns[k], 256)
            part = lax.dot_general(
                w_ref[:, cols], table[:, cols], (((1,), (1,)), ((), ())), preferred_element_type=jnp.float32
            )
            if k == 0:
                hidden[...] = part
            else:
                hidden[...] += part
        for load in load_c:
            load.wait()
        for at in range(0, rows, block):
            cols = slice(at, at + block)
            factor = slope(hidden[:, cols], scale, root_0 / tokens)
            for m in range(8):
                span = slice(m * units, (m + 1) * units)
                up[span, cols] = (cot[span, cols].astype(jnp.float32) * factor).astype(jnp.bfloat16)
        load_c = load_cots(1)

        @pl.loop(0, width // wide)
        def _(i):
            cols = pl.ds(pl.multiple_of(i * wide, wide), wide)
            halves = [jnp.dot(up[at, :], table[:, cols], preferred_element_type=jnp.float32) for at in half]
            kept = w_ref[:, cols].astype(jnp.float32) * keep
            total = jnp.zeros(kept.shape, jnp.float32)
            for m in range(8):
                span = slice(m * units, (m + 1) * units)
                g = halves[m // 4][m % 4 * units : (m % 4 + 1) * units]
                r = g * pl.reciprocal(jnp.abs(g) + eps * root_0, approx=True)
                total = total + r
                work[span, cols] = (kept - inner_rate * r).astype(jnp.bfloat16)
                grads[span, cols] = g.astype(jnp.bfloat16)
            ratio[:, cols] = total

        for load in load_c:
            load.wait()

        @pl.loop(0, rows // block)
        def _(t):
            at = pl.ds(pl.multiple_of(t * block, block), block)
            products = [
                lax.dot_general(
                    work[rows_of, :], table[at, :], (((1,), (1,)), ((), ())), preferred_element_type=jnp.float32
                )
                for rows_of in half
            ]
            for rows_of, product in zip(half, products):
                up[rows_of, at] = (cot[rows_of, at].astype(jnp.float32) * slope(product, scale, root_1 / tokens)).astype(
                    jnp.bfloat16
                )

        load_m.wait()

        @pl.loop(0, width // wide)
        def _(i):
            cols = pl.ds(pl.multiple_of(i * wide, wide), wide)
            halves = [jnp.dot(up[at, :], table[:, cols], preferred_element_type=jnp.float32) for at in half]
            start_w = w_ref[:, cols].astype(jnp.float32)
            total = jnp.zeros(start_w.shape, jnp.float32)
            for m in range(8):
                span = slice(m * units, (m + 1) * units)
                b = halves[m // 4][m % 4 * units : (m % 4 + 1) * units].astype(narrow)
                a = grads[span, cols]
                v = a * a + b * b + narrow(1e-30)
                r = (a + narrow(weight_1 / weight_0) * b) * pl.reciprocal(
                    v * lax.rsqrt(v) + narrow(eps), approx=True
                )
                total = total + r.astype(jnp.float32)
            mean = (1.0 - keep * keep) * start_w + (inner_rate / 8.0) * (keep * ratio[:, cols] + weight_0 * total)
            moment = outer_moment * mom_ref[:, cols].astype(jnp.float32) + mean
            out_ref[:, cols] = (start_w - outer_rate * (mean + outer_moment * moment)).astype(jnp.bfloat16)

    return pl.pallas_call(
        kernel,
        in_specs=[pl.BlockSpec(memory_space=pltpu.SMEM)] + [pl.BlockSpec(memory_space=pltpu.HBM)] * (n + 2 + 2 * sets),
        out_specs=pl.BlockSpec(memory_space=pltpu.VMEM),
        out_shape=jax.ShapeDtypeStruct((units, width), jnp.bfloat16),
        scratch_shapes=[
            pltpu.VMEM((rows, width), jnp.bfloat16),
            pltpu.VMEM((many, width), jnp.bfloat16),
            pltpu.VMEM((many, width), jnp.bfloat16),
            pltpu.VMEM((many, rows), jnp.bfloat16),
            pltpu.VMEM((many, rows), jnp.bfloat16),
            pltpu.VMEM((units, width), jnp.float32),
            pltpu.VMEM((units, rows), jnp.float32),
            pltpu.VMEM((units, width), jnp.bfloat16),
            pltpu.VMEM((units, width), jnp.bfloat16),
            pltpu.SemaphoreType.DMA((16,)),
            pltpu.SemaphoreType.DMA((2 + sets,)),
        ],
        compiler_params=pltpu.CompilerParams(vmem_limit_bytes=VMEM_ALL),
        cost_estimate=pl.CostEstimate(flops=52 * units * rows * width, bytes_accessed=rows * width * 2, transcendentals=0),
        name="main_steps",
    )(position, *pieces, w, momentum, *(c for pair in cots for c in pair))


def spread(new):
    e1, e2, e3 = LINKS
    near = [over_island(new, e) for e in LINKS]
    far = [over_island(near[1], e1), over_island(near[2], e2), over_island(near[0], e3)]
    found = [(new, 0), (near[0], e1), (near[1], e2), (near[2], e3)]
    found += [(far[0], e1 ^ e2), (far[1], e2 ^ e3), (far[2], e1 ^ e3)]
    last = []
    for (low, size), source, e in zip(PARTS, (far[1], far[2], far[0]), LINKS):
        last.append((over_island(source[:, low : low + size], e), low))
    return found, last


def assemble(found, where, units, width):
    n = len(found)

    def kernel(where_ref, *refs):
        arrays, out, held, turned, sems, out_sems = refs[:n], *refs[n:]
        waits = []
        for p, (low, length) in enumerate(TURNS):
            copies = []
            for k, (_, mask) in enumerate(found):
                row = row_of(where_ref, mask, units)
                part = pl.ds(low, length)
                copy = pltpu.make_async_copy(
                    arrays[k].at[:, part], held.at[pl.ds(row, units), part], sems.at[p, k]
                )
                copy.start()
                copies.append(copy)
            waits.append(copies)
        row = row_of(where_ref, LAST, units)
        held[pl.ds(row, units), :] = jnp.zeros((units, width), held.dtype)
        outs = []
        for p, (low, length) in enumerate(TURNS):
            for copy in waits[p]:
                copy.wait()
            for col in range(low, low + length, 128):
                turned[col : col + 128, :] = held[:, col : col + 128].T
            copy = pltpu.make_async_copy(
                turned.at[pl.ds(low, length), :], out.at[pl.ds(low, length), :], out_sems.at[p]
            )
            copy.start()
            outs.append(copy)
        for copy in outs:
            copy.wait()

    return pl.pallas_call(
        kernel,
        in_specs=[pl.BlockSpec(memory_space=pltpu.SMEM)] + [pl.BlockSpec(memory_space=pl.ANY)] * n,
        out_specs=pl.BlockSpec(memory_space=pltpu.HBM),
        out_shape=jax.ShapeDtypeStruct((width, 8 * units), jnp.bfloat16),
        scratch_shapes=[
            pltpu.VMEM((8 * units, width), jnp.bfloat16),
            pltpu.VMEM((width, 8 * units), jnp.bfloat16),
            pltpu.SemaphoreType.DMA((len(TURNS), n)),
            pltpu.SemaphoreType.DMA((len(TURNS),)),
        ],
        compiler_params=pltpu.CompilerParams(vmem_limit_bytes=24 * MB),
        cost_estimate=pl.CostEstimate(flops=0, bytes_accessed=32 * units * width, transcendentals=0),
        name="assemble",
    )(where, *(array for array, _ in found))


def complete(whole, last, where, units, width):
    n = len(last)
    window = 256

    def kernel(where_ref, whole_ref, *refs):
        arrays, out, kept, held, merged, in_sems, sems, out_sems = refs[:n], *refs[n:]
        low, shift = window_of(where_ref, LAST, units)
        cols = pl.ds(low, window)
        loads, arrivals = [], []
        for k, (array, low) in enumerate(last):
            part = pl.ds(low, array.shape[1])
            arrival = pltpu.make_async_copy(arrays[k], held.at[pl.ds(shift, units), part], sems.at[k])
            arrival.start()
            arrivals.append(arrival)
        for p, (low, length) in enumerate(TURNS):
            part = pl.ds(low, length)
            load = pltpu.make_async_copy(whole_ref.at[part, cols], kept.at[part, :], in_sems.at[p])
            load.start()
            loads.append(load)
        lane = lax.broadcasted_iota(jnp.int32, (128, window), 1)
        ours = (lane >= shift) & (lane < shift + units)
        stores = []
        for p, (low, length) in enumerate(TURNS):
            loads[p].wait()
            if low in [first for _, first in last]:
                arrivals[[first for _, first in last].index(low)].wait()
            for col in range(low, low + length, 128):
                here = slice(col, col + 128)
                merged[here, :] = jnp.where(ours, held[:, here].T.astype(jnp.float32), kept[here, :].astype(jnp.float32)).astype(
                    merged.dtype
                )
            part = pl.ds(low, length)
            store = pltpu.make_async_copy(merged.at[part, :], out.at[part, cols], out_sems.at[p])
            store.start()
            stores.append(store)
        for store in stores:
            store.wait()

    return pl.pallas_call(
        kernel,
        in_specs=[pl.BlockSpec(memory_space=pltpu.SMEM), pl.BlockSpec(memory_space=pltpu.HBM)]
        + [pl.BlockSpec(memory_space=pl.ANY)] * n,
        out_specs=pl.BlockSpec(memory_space=pltpu.HBM),
        out_shape=jax.ShapeDtypeStruct(whole.shape, whole.dtype),
        input_output_aliases={1: 0},
        scratch_shapes=[
            pltpu.VMEM((width, window), whole.dtype),
            pltpu.VMEM((window, width), whole.dtype),
            pltpu.VMEM((width, window), whole.dtype),
            pltpu.SemaphoreType.DMA((len(TURNS),)),
            pltpu.SemaphoreType.DMA((n,)),
            pltpu.SemaphoreType.DMA((len(TURNS),)),
        ],
        compiler_params=pltpu.CompilerParams(vmem_limit_bytes=16 * MB),
        cost_estimate=small(),
        name="complete",
    )(where, whole, *(array for array, _ in last))


def body(weights, momentum, table, token_ids, cotangent):
    island, fsdp = lax.axis_index("island"), lax.axis_index("fsdp")
    width, hidden_units = weights.shape
    steps, tokens = token_ids.shape[1:]
    rows = table.shape[0]
    units = hidden_units // 8
    where = jnp.stack([island, fsdp]).astype(jnp.int32)

    def exchange(k):
        return over_island(m[k], MASKS[0][k], MASKS[1][k])

    z, x1, x2 = over_z(table), over_x(table, True), over_x(table, False)
    m = list(turn_cotangent(where, cotangent[0], token_ids[0]))
    w, mom = own_rows(where, weights, momentum, m[:1])
    k1, k2 = exchange(1), exchange(2)
    z, x1, x2, k1, k2, w, mom, *m[3:] = together(z, x1, x2, k1, k2, w, mom, *m[3:])

    x1z, x3, x2z, k3 = over_z(x1), over_x(x1, False), over_x(z, False), exchange(3)
    x1_o = over_core(x1)
    c0, c1 = add_by_row([m[0], k1, k2], rows, steps)
    k3, x1_o, m[4], m[5] = together(k3, x1_o, m[4], m[5])
    k4, k5 = exchange(4), exchange(5)
    early = pack([table, x2, z])
    x1z, x3, x2z, k4, k5, early, c0, c1, *m[6:] = together(x1z, x3, x2z, k4, k5, early, c0, c1, *m[6:])
    cots = [(c0, c1)]

    x3z, k6, k7, early_o = over_x(x1z, False), exchange(6), exchange(7), over_core(early)
    x3_o = over_core(x3)
    c0, c1 = add_by_row([k3, k4, k5], rows, steps)
    x3z, k6, k7, early_o, x3_o, c0, c1 = together(x3z, k6, k7, early_o, x3_o, c0, c1)
    cots.append((c0, c1))

    others = [early_o, x1_o, x3_o, over_core(x1z), over_core(x2z), over_core(x3z)]
    cots.append(add_by_row([k6, k7], rows, steps))
    pieces = [table, x1, x2, z, x3, x1z, x2z, x3z, *others]
    new = main_steps(pieces, where, w, mom, cots, tokens)
    found, last = spread(new)
    return complete(assemble(found, where, units, width), last, where, units, width)


def solution(mesh):
    placed = (
        P(None, "fsdp"),
        P(None, "fsdp"),
        P(None, "fsdp"),
        P("island", None, None),
        P("island", None, None, "fsdp"),
    )
    return jax.shard_map(body, mesh=mesh, in_specs=placed, out_specs=P(None, "fsdp"), check_vma=False)
```
